256 devices in a mesh: row: 16 (over y, x_hi, core), col: 16 (over x_lo, z).
Axes of the slice: x: 4 (x_hi: 2, x_lo: 2; x = x_hi * 2 + x_lo), y: 4, z: 8, core: 2. Of those that a mesh axis runs over, the one named last changes fastest.
Arguments:
- amplitudes: float32 [2048, 2048], P('row', 'col'), may hold values from -6 to 6
- integrals: float32 [2048, 163840], P(None, ('row', 'col')), may hold values from -3 to 3, as said below
- occ_irrep: int32 [2048], replicated, may hold values from 0 to 7, as said below
- cd_irrep: int32 [2048], P('col'), may hold values from 0 to 7
- vir_irrep: int32 [163840], P(('row', 'col')), may hold values from 0 to 7, as said below
- occ_energy: float32 [2048], replicated, may hold values from -4 to -1, as said below
- vir_energy: float32 [163840], P(('row', 'col')), may hold values from 1 to 6, as said below
Outputs:
- update: float32 [2048, 163840], P(None, ('row', 'col'))
The draws below stay inside these ranges and needn't reach their ends.
Inputs may be any that keep to these rules, and one draw needn't show every extreme that they name: `occ_irrep`: entry p equals entry p + 2048/2 (a pair and its mirror share their irrep). `vir_irrep`: entry q equals entry q + 81920. `occ_energy`: entry p equals entry p + 1024. `vir_energy`: entry q equals entry q + 81920. `integrals`: column q + 81920 is exactly minus column q (antisymmetry in ab).
All inputs are finite; a program needn't handle non-finite values.
Results may differ from the reference program's by a relative error of at most 0.000088.
Values sent between devices are 32-bit elements; how exact they have to be, the bound alone decides.
No kernel may reach another device: no remote copies, remote signals or barrier semaphores. Data moves between devices by JAX's collectives and lax.ppermute only.
A program may use at most 128 MiB of HBM per device.

```python
import jax
import jax.numpy as jnp
from jax import lax

SLAB = 2048
VPAIRS = 163840
PAIRS = 2048


def doubled(values):
    return jnp.concatenate([values, values], axis=0)


def draw_occ_irrep(key, part):
    key = jax.random.fold_in(key, 11)
    return doubled(jax.random.randint(key, (PAIRS // 2,), 0, 8)).astype(jnp.int32)


def draw_vir_irrep(key, part):
    key = jax.random.fold_in(key, 13)
    return doubled(jax.random.randint(key, (VPAIRS // 2,), 0, 8)).astype(jnp.int32)


def draw_occ_energy(key, part):
    key = jax.random.fold_in(key, 17)
    base = jax.random.uniform(key, (PAIRS // 2,), jnp.float32, 0.0, 1.0)
    values = -1.0 - 3.0 * base
    return doubled(values).astype(jnp.float32)


def draw_vir_energy(key, part):
    key = jax.random.fold_in(key, 19)
    base = jax.random.uniform(key, (VPAIRS // 2,), jnp.float32, 0.0, 1.0)
    values = 1.0 + 5.0 * base
    return doubled(values).astype(jnp.float32)


def draw_integrals(key, part):
    key = jax.random.fold_in(key, 23)
    half = jnp.clip(0.5 * jax.random.normal(key, (SLAB, VPAIRS // 2), jnp.float32), -3.0, 3.0)
    return jnp.concatenate([half, -half], axis=1).astype(jnp.float32)


def place_ends(entries, rng, smallest, largest):
    longest = entries.shape.index(max(entries.shape))
    spots = []
    for shift in (0, 1):
        where = [jax.random.randint(jax.random.fold_in(rng, axis), (), 0, length) for axis, length in enumerate(entries.shape)]
        where[longest] = (where[longest] + shift) % entries.shape[longest]
        spots.append(tuple(where))
    return entries.at[spots[0]].set(smallest).at[spots[1]].set(largest)


def shard_levels(stream_key, extent, cuts, smallest, largest):
    level = 1.0
    for dim, shards_of in cuts:
        heights = jax.random.uniform(jax.random.fold_in(jax.random.fold_in(stream_key, 6), dim), (shards_of,), jnp.float32, smallest / len(cuts), largest / len(cuts))
        level = level * jnp.repeat(jnp.exp(heights), extent[dim] // shards_of).reshape((-1,) + (1,) * (len(extent) - 1 - dim))
    return level


def noise(stream_key, dims, scale, most, split=(), kind=jnp.bfloat16):
    entries = scale * jax.random.normal(stream_key, dims, jnp.float32)
    if split:
        entries = entries * shard_levels(stream_key, dims, split, -0.22, 0.18)
    return jnp.clip(entries, -most, most).astype(kind)


def setup_inputs(seed: int = 0) -> dict:
    key_list = jax.random.split(jax.random.key(seed), 8)
    return {
        "amplitudes": noise(key_list[0], (PAIRS, SLAB), 1.0, 6.0, ((0, 16), (1, 16)), jnp.float32),
        "integrals": draw_integrals(jax.random.fold_in(key_list[7], 71), 0),
        "occ_irrep": draw_occ_irrep(jax.random.fold_in(key_list[7], 71), 0),
        "cd_irrep": place_ends(jax.random.randint(key_list[3], (SLAB,), 0, 8), jax.random.fold_in(key_list[3], 1), 0, 7).astype(jnp.int32),
        "vir_irrep": draw_vir_irrep(jax.random.fold_in(key_list[7], 71), 0),
        "occ_energy": draw_occ_energy(jax.random.fold_in(key_list[7], 71), 0),
        "vir_energy": draw_vir_energy(jax.random.fold_in(key_list[7], 71), 0),
    }


def reference(amplitudes, integrals, occ_irrep, cd_irrep, vir_irrep, occ_energy, vir_energy):
    highest = lax.Precision.HIGHEST
    match = (occ_irrep[:, None] == cd_irrep[None, :]).astype(amplitudes.dtype)
    masked_t = amplitudes * match
    half = VPAIRS // 2
    shift_rows = PAIRS // 2

    def ladder_half(lower):
        cols = integrals[:, lower:lower + half]
        keep = (cd_irrep[:, None] == vir_irrep[None, lower:lower + half]).astype(integrals.dtype)
        return jnp.dot(masked_t, cols * keep, precision=highest, preferred_element_type=jnp.float32)

    first = ladder_half(0)
    second = ladder_half(half)
    denom_first = occ_energy[:, None] - vir_energy[None, :half]
    denom_second = occ_energy[:, None] - vir_energy[None, half:]
    out_first = 0.5 * (first + jnp.roll(second, shift_rows, axis=0)) / denom_first
    out_second = 0.5 * (second + jnp.roll(first, shift_rows, axis=0)) / denom_second
    return jnp.concatenate([out_first, out_second], axis=1)
```

```python
import functools

import jax
import jax.numpy as jnp
from jax import lax
from jax.experimental import pallas as pl
from jax.experimental.pallas import tpu as pltpu
from jax.sharding import PartitionSpec as P

BLOCK = 128
IRREPS = 8
HALF = 16
SLOTS = 2 * HALF
BLOCKS = 8
META = 8

COL_BITS = (4, 2, 1, 8)
ROW_BITS = (2, 4)

f32, bf16, i32 = jnp.float32, jnp.bfloat16, jnp.int32
MIB = 1 << 20


def iota(shape, dim):
    return lax.broadcasted_iota(i32, shape, dim)


def strict_upper():
    return jnp.where(iota((BLOCK, BLOCK), 0) < iota((BLOCK, BLOCK), 1), 1.0, 0.0).astype(bf16)


def mm(a, b):
    return jnp.dot(a, b, preferred_element_type=f32)


def high_low(x):
    high = x.astype(bf16)
    return high, (x - high.astype(f32)).astype(bf16)


def pack_kernel(base_ref, amp_ref, occ_ref, cd_ref, keep_ref, send_ref):
    row = lax.axis_index("row")
    half = row // BLOCKS
    block = row % BLOCKS
    occ = occ_ref[pl.ds(block, 1), :]
    same = jnp.where(occ == iota((IRREPS, BLOCK), 0), 1.0, 0.0)
    ranks = mm(same.astype(bf16), strict_upper())
    rank = jnp.sum(same * ranks, axis=0, keepdims=True).astype(i32)
    key = occ * BLOCK + rank - base_ref[0] * SLOTS
    line = iota((2 * BLOCK, BLOCK), 0)
    wanted = ((line >> 4) & 7) * BLOCK + 2 * (line & 15) + (line >> 7)
    pick = jnp.where(key == wanted, 1.0, 0.0).astype(bf16)
    amp = amp_ref[...]
    first = amp.astype(bf16)
    rest = amp - first.astype(f32)
    second = rest.astype(bf16)
    third = (rest - second.astype(f32)).astype(bf16)
    packed = mm(pick, first) + mm(pick, second) + mm(pick, third)
    cd = cd_ref[...]
    sign = (1 - 2 * half).astype(f32)
    sides = []
    for side in range(2):
        total = jnp.zeros((HALF, BLOCK), f32)
        for g in range(IRREPS):
            lines = packed[side * BLOCK + g * HALF : side * BLOCK + (g + 1) * HALF]
            total = total + jnp.where(cd == g, lines, 0.0)
        sides.append(sign * total)
    lower = half == 0
    keep_ref[:HALF, :] = jnp.where(lower, sides[0], sides[1])
    send_ref[:HALF, :] = jnp.where(lower, sides[1], sides[0])
    keep_ref[HALF:, :] = jnp.broadcast_to(cd.astype(f32), (META, BLOCK))
    send_ref[HALF:, :] = jnp.zeros((META, BLOCK), f32)


def table_kernel(base_ref, occ_ref, energy_ref, vir_ref, vir_energy_ref, scale_ref, rows_ref, passes_ref):
    half = lax.axis_index("row") // BLOCKS
    occ = occ_ref[:BLOCKS, :]
    energy = energy_ref[:BLOCKS, :]
    irrep = iota((IRREPS, BLOCK), 0)
    same = jnp.concatenate(
        [jnp.where(occ[b : b + 1] == irrep, 1.0, 0.0) for b in range(BLOCKS)], axis=0
    )
    ranks = mm(same.astype(bf16), strict_upper())
    counts = jnp.sum(same, axis=1, keepdims=True)
    most = jnp.max(counts).astype(i32)
    passes_ref[0] = (most + SLOTS - 1) // SLOTS
    rank = jnp.concatenate(
        [
            jnp.sum((same * ranks)[b * IRREPS : (b + 1) * IRREPS], axis=0, keepdims=True)
            for b in range(BLOCKS)
        ],
        axis=0,
    ).astype(i32) - base_ref[0] * SLOTS
    both = jnp.concatenate(
        [occ.astype(f32), rank.astype(f32), jnp.zeros((BLOCK - 2 * BLOCKS, BLOCK), f32)], axis=0
    )
    rows_ref[...] = both.T
    key = occ * BLOCK + rank
    line = iota((BLOCK, BLOCK), 0)
    wanted = (line >> 4) * BLOCK + 2 * (line & 15) + half
    vir = vir_ref[...]
    vir_energy = vir_energy_ref[...]
    for b in range(BLOCKS):
        found = jnp.sum(
            jnp.where(key[b : b + 1] == wanted, energy[b : b + 1], 0.0), axis=1, keepdims=True
        )
        at_slot = jnp.zeros((HALF, vir.shape[1]), f32)
        for g in range(IRREPS):
            at_slot = at_slot + jnp.where(vir == g, found[g * HALF : (g + 1) * HALF], 0.0)
        scale_ref[b * HALF : (b + 1) * HALF, :] = 0.5 / (at_slot - vir_energy)


def ladder_kernel(own_ref, other_ref, meta_ref, scale_ref, vir_ref, v_ref, out_ref, held, sems):
    row = lax.axis_index("row")
    col = lax.axis_index("col")
    count = held.shape[0]

    def mask_of(bits, index):
        return sum(bit for place, bit in enumerate(bits) if index >> place & 1)

    copies = []
    for j in range(count):
        start = pl.multiple_of((col ^ mask_of(COL_BITS, j)) * BLOCK, BLOCK)
        copies.append(pltpu.make_async_copy(v_ref.at[pl.ds(start, BLOCK)], held.at[j], sems.at[j]))
        copies[-1].start()
    meta = jnp.concatenate(
        [meta_ref[j, HALF : HALF + 1, :] for j in range(count)]
        + [jnp.zeros((BLOCK - count, BLOCK), f32)],
        axis=0,
    ).T
    vir = vir_ref[...].astype(f32)
    rows = BLOCKS // 2
    total = None
    group = 4
    for j0 in range(0, count, group):
        left, right = [], []
        for j in range(j0, j0 + group):
            copies[j].wait()
            right.append(jnp.where(meta[:, j : j + 1] == vir, held[j], 0.0))
            left.append(
                jnp.concatenate(
                    [own_ref[r * count + j] for r in range(rows)]
                    + [other_ref[r * count + j] for r in range(rows)],
                    axis=0,
                )
            )
        a_high, a_low = high_low(jnp.concatenate(left, axis=1))
        b_high, b_low = high_low(jnp.concatenate(right, axis=0))
        twice = mm(jnp.concatenate([a_high, a_low], axis=0), b_high)
        term = twice[:BLOCK] + twice[BLOCK:] + mm(a_high, b_low)
        total = term if total is None else total + term
    me = row % BLOCKS
    for side in range(2):
        for r in range(rows):
            place = pl.multiple_of((me ^ mask_of(ROW_BITS, r) ^ side) * HALF, HALF)
            line = (side * rows + r) * HALF
            lines = pl.ds(place, HALF)
            out_ref[lines, :] = total[line : line + HALF] * scale_ref[lines, :]


def expand_kernel(own_ref, other_ref, rows_ref, vir_ref, out_ref, held, sems):
    half = lax.axis_index("row") // BLOCKS
    lane = iota((1, 2 * SLOTS), 1)
    mine = (lane & HALF) == 0
    wanted = 2 * (lane & 15) + jnp.where(mine, half, 1 - half)
    sign = jnp.where(mine, 1.0, -1.0)
    vir = vir_ref[...].astype(f32)
    wanted = wanted.astype(f32)
    copies = []
    for b in range(BLOCKS):
        slots = slice(b * HALF, (b + 1) * HALF)
        packed = jnp.concatenate([own_ref[slots, :], other_ref[slots, :]], axis=0)
        high, low = high_low(packed)
        pick = jnp.where(rows_ref[:, BLOCKS + b : BLOCKS + b + 1] == wanted, sign, 0.0).astype(bf16)
        spread = mm(pick, jnp.concatenate([high, low], axis=0))
        spread = jnp.where(rows_ref[:, b : b + 1] == vir, spread, 0.0)
        held[0, b] = spread
        held[1, b] = -spread
        for side in range(2):
            copies.append(
                pltpu.make_async_copy(held.at[side, b], out_ref.at[side, b], sems.at[side, b])
            )
            copies[-1].start()
    for copy in copies:
        copy.wait()


VMEM = pl.BlockSpec(memory_space=pltpu.VMEM)
SMEM = pl.BlockSpec(memory_space=pltpu.SMEM)
ANY = pl.BlockSpec(memory_space=pl.ANY)


def params(mib):
    return pltpu.CompilerParams(vmem_limit_bytes=mib * MIB)


def swapped(x, axis, bit):
    return lax.ppermute(x, axis, [(i, i ^ bit) for i in range(lax.axis_size(axis))])


def one_pass(base, amplitudes, integrals, occ, cd, vir, energy, vir_energy):
    depth, width = integrals.shape
    cols = depth // BLOCK
    shape = jax.ShapeDtypeStruct
    lines = HALF + META
    keep, send = pl.pallas_call(
        pack_kernel,
        out_shape=[shape((lines, BLOCK), f32)] * 2,
        in_specs=[SMEM, VMEM, VMEM, VMEM],
        out_specs=[VMEM, VMEM],
        compiler_params=params(8),
    )(base, amplitudes, occ, cd)
    scale, rows, passes = pl.pallas_call(
        table_kernel,
        out_shape=[
            shape((BLOCKS * HALF, width), f32),
            shape((BLOCK, BLOCK), f32),
            shape((1,), i32),
        ],
        in_specs=[SMEM, VMEM, VMEM, VMEM, VMEM],
        out_specs=[VMEM, VMEM, SMEM],
        compiler_params=params(8),
        cost_estimate=pl.CostEstimate(flops=4000000, bytes_accessed=500000, transcendentals=0),
    )(base, occ, energy, vir, vir_energy)
    x = (keep + swapped(send, "row", BLOCKS))[None]
    for bit in COL_BITS:
        x = jnp.concatenate([x, swapped(x, "col", bit)], axis=0)
    meta = x
    x = x[:, :HALF]
    for bit in ROW_BITS:
        x = jnp.concatenate([x, swapped(x, "row", bit)], axis=0)
    other = swapped(x, "row", 1)
    ladder = pl.pallas_call(
        ladder_kernel,
        out_shape=shape((BLOCKS * HALF, width), f32),
        in_specs=[VMEM, VMEM, VMEM, VMEM, VMEM, ANY],
        out_specs=VMEM,
        scratch_shapes=[
            pltpu.VMEM((cols, BLOCK, width), f32),
            pltpu.SemaphoreType.DMA((cols,)),
        ],
        compiler_params=params(32),
        cost_estimate=pl.CostEstimate(
            flops=6 * BLOCK * depth * width, bytes_accessed=4 * depth * width, transcendentals=0
        ),
    )(x, other, meta, scale, vir, integrals)
    mirrored = swapped(ladder, "row", BLOCKS)
    out = pl.pallas_call(
        expand_kernel,
        out_shape=shape((2, BLOCKS, BLOCK, width), f32),
        in_specs=[VMEM, VMEM, VMEM, VMEM],
        out_specs=ANY,
        scratch_shapes=[
            pltpu.VMEM((2, BLOCKS, BLOCK, width), f32),
            pltpu.SemaphoreType.DMA((2, BLOCKS)),
        ],
        compiler_params=params(32),
    )(ladder, mirrored, rows, vir)
    return out, passes[0]


def local(amplitudes, integrals, occ_irrep, cd_irrep, vir_irrep, occ_energy, vir_energy):
    run = functools.partial(
        one_pass,
        amplitudes=amplitudes,
        integrals=integrals,
        occ=occ_irrep.reshape(-1, BLOCK),
        cd=cd_irrep.reshape(1, -1),
        vir=vir_irrep.reshape(1, -1),
        energy=occ_energy.reshape(-1, BLOCK),
        vir_energy=vir_energy.reshape(1, -1),
    )
    out, passes = run(jnp.zeros((1,), i32))

    def more(state):
        return state[0] < passes

    def step(state):
        index, total = state
        extra, _ = run(jnp.full((1,), index, i32))
        return index + 1, total + extra

    _, out = lax.while_loop(more, step, (jnp.int32(1), out))
    return out.reshape(occ_irrep.shape[0], -1)


def solution(mesh):
    in_specs = (
        P("row", "col"),
        P(None, ("row", "col")),
        P(),
        P("col"),
        P(("row", "col")),
        P(),
        P(("row", "col")),
    )
    out_specs = P(None, ("row", "col"))
    return jax.shard_map(local, mesh=mesh, in_specs=in_specs, out_specs=out_specs, check_vma=False)
```

```python
import functools

import jax
import jax.numpy as jnp
from jax import lax
from jax.experimental import pallas as pl
from jax.experimental.pallas import tpu as pltpu
from jax.sharding import Mesh
from jax.sharding import PartitionSpec as P

BLOCK = 128
IRREPS = 8
HALF = 16
META = 8
SLOTS = 2 * HALF
BLOCKS = 8
COLS = 16
PART = BLOCKS // 2

ROW = ("yh", "yl", "xh", "core")
COL = ("xl", "z2", "z1", "z0")

NEAR = ("yh", "yl", "xl")
COL_STEPS = (("z2", "z1"), ("z1",), ("z0",))
X_STEP = ("xh", "xl")

f32, bf16, i32 = jnp.float32, jnp.bfloat16, jnp.int32
MIB = 1 << 20


def iota(shape, dim):
    return lax.broadcasted_iota(i32, shape, dim)


def strict_upper():
    return jnp.where(iota((BLOCK, BLOCK), 0) < iota((BLOCK, BLOCK), 1), 1.0, 0.0).astype(bf16)


def mm(a, b):
    return jnp.dot(a, b, preferred_element_type=f32)


def high_low(x):
    high = x.astype(bf16)
    return high, (x - high.astype(f32)).astype(bf16)


def number(axes):
    total = 0
    for axis in axes:
        total = 2 * total + lax.axis_index(axis)
    return total


def own_block():
    return number(ROW[1:])


def other_block(index):
    xh = lax.axis_index("xh") ^ (index >> 2)
    core = lax.axis_index("core") ^ (index >> 1 & 1)
    return (index & 1) * 4 + xh * 2 + core


def other_col(index):
    mask = 0
    for place, step in enumerate(COL_STEPS):
        if index >> 1 + place & 1:
            mask ^= sum(1 << (len(COL) - 1 - COL.index(axis)) for axis in step)
    return (index & 1) * 8 + (number(COL[1:]) ^ mask)


def rank_of(slot, upper):
    return 2 * slot + upper


def flat(ref):
    return jnp.concatenate([ref[i : i + 1, :] for i in range(ref.shape[0])], axis=1)


def pack_kernel(base_ref, amp_ref, occ_ref, cd_ref, out_ref):
    upper = lax.axis_index("yh")
    y = number(("yh", "yl"))
    occ = occ_ref[pl.ds(own_block(), 1), :]
    same = jnp.where(occ == iota((IRREPS, BLOCK), 0), 1.0, 0.0)
    ranks = mm(same.astype(bf16), strict_upper())
    rank = jnp.sum(same * ranks, axis=0, keepdims=True).astype(i32)
    key = occ * BLOCK + rank - base_ref[0] * SLOTS
    line = iota((2 * BLOCK, BLOCK), 0)
    wanted = ((line >> 4) & 7) * BLOCK + rank_of(line & 15, line >> 7)
    pick = jnp.where(key == wanted, 1.0, 0.0).astype(bf16)
    amp = amp_ref[...]
    first = amp.astype(bf16)
    rest = amp - first.astype(f32)
    second = rest.astype(bf16)
    third = (rest - second.astype(f32)).astype(bf16)
    packed = mm(pick, first) + mm(pick, second) + mm(pick, third)
    cd = cd_ref[...]
    sign = (1 - 2 * upper).astype(f32)
    tile = jnp.where(iota((META, BLOCK), 0) == number(COL[1:]), cd.astype(f32), 0.0)
    for side in range(2):
        total = jnp.zeros((HALF, BLOCK), f32)
        for g in range(IRREPS):
            lines = packed[side * BLOCK + g * HALF : side * BLOCK + (g + 1) * HALF]
            total = total + jnp.where(cd == g, lines, 0.0)
        total = sign * total
        for yl in range(2):
            mine = jnp.where(y == 2 * side + yl, tile, 0.0)
            for xl in range(2):
                place = 4 * side + 2 * yl + xl
                out_ref[place, :HALF, :] = total
                out_ref[place, HALF:, :] = mine


def table_kernel(
    base_ref, occ_ref, energy_ref, vir_ref, vir_energy_ref, scale_ref, rows_ref, token_ref, passes_ref
):
    token_ref[...] = jnp.zeros(token_ref.shape, f32)
    upper = lax.axis_index("yh")

    def ordered(ref):
        return jnp.concatenate(
            [ref[pl.ds(other_block(i), 1), :] for i in range(BLOCKS)], axis=0
        )

    occ = ordered(occ_ref)
    energy = ordered(energy_ref)
    irrep = iota((IRREPS, BLOCK), 0)
    same = jnp.concatenate(
        [jnp.where(occ[b : b + 1] == irrep, 1.0, 0.0) for b in range(BLOCKS)], axis=0
    )
    ranks = mm(same.astype(bf16), strict_upper())
    counts = jnp.sum(same, axis=1, keepdims=True)
    most = jnp.max(counts).astype(i32)
    passes_ref[0] = (most + SLOTS - 1) // SLOTS
    rank = jnp.concatenate(
        [
            jnp.sum((same * ranks)[b * IRREPS : (b + 1) * IRREPS], axis=0, keepdims=True)
            for b in range(BLOCKS)
        ],
        axis=0,
    ).astype(i32) - base_ref[0] * SLOTS
    both = jnp.concatenate(
        [occ.astype(f32), rank.astype(f32), jnp.zeros((BLOCK - 2 * BLOCKS, BLOCK), f32)], axis=0
    )
    rows_ref[...] = both.T
    key = occ * BLOCK + rank
    line = iota((BLOCK, BLOCK), 0)
    wanted = (line >> 4) * BLOCK + rank_of(line & 15, upper)
    vir = flat(vir_ref)
    vir_energy = flat(vir_energy_ref)
    for b in range(BLOCKS):
        found = jnp.sum(
            jnp.where(key[b : b + 1] == wanted, energy[b : b + 1], 0.0), axis=1, keepdims=True
        )
        at_slot = jnp.zeros((HALF, vir.shape[1]), f32)
        for g in range(IRREPS):
            at_slot = at_slot + jnp.where(vir == g, found[g * HALF : (g + 1) * HALF], 0.0)
        scale_ref[b * HALF : (b + 1) * HALF, :] = 0.5 / (at_slot - vir_energy)


def load_kernel(v_ref, out_ref, token_ref, sems):
    token_ref[...] = jnp.zeros(token_ref.shape, f32)
    copies = []
    for j in range(COLS):
        start = pl.multiple_of(other_col(j) * BLOCK, BLOCK)
        copies.append(pltpu.make_async_copy(v_ref.at[pl.ds(start, BLOCK)], out_ref.at[j], sems.at[j]))
        copies[-1].start()
    for copy in copies:
        copy.wait()


def split_kernel(meta_ref, vir_ref, held_ref, high_ref, low_ref, token_ref):
    token_ref[...] = jnp.zeros(token_ref.shape, f32)
    meta = jnp.concatenate(
        [meta_ref[pl.ds(other_col(j), 1), :] for j in range(COLS)]
        + [jnp.zeros((BLOCK - COLS, BLOCK), f32)],
        axis=0,
    ).T
    vir = flat(vir_ref).astype(f32)
    for j in range(COLS):
        high, low = high_low(jnp.where(meta[:, j : j + 1] == vir, held_ref[j], 0.0))
        high_ref[j * BLOCK : (j + 1) * BLOCK, :] = high
        low_ref[j * BLOCK : (j + 1) * BLOCK, :] = low


def ladder_kernel(side, near_ref, far_ref, high_ref, low_ref, scale_ref, *refs):
    out_ref, token_ref = refs[-2:]
    token_ref[...] = jnp.zeros(token_ref.shape, f32)
    lines = PART * HALF
    total = None
    group = 4
    for j0 in range(0, COLS, group):
        left = [
            jnp.concatenate(
                [
                    ref[(j >> 1) * 4 + 2 * yl + (j & 1)]
                    for ref in (near_ref, far_ref)
                    for yl in range(2)
                ],
                axis=0,
            )
            for j in range(j0, j0 + group)
        ]
        depth = slice(j0 * BLOCK, (j0 + group) * BLOCK)
        a_high, a_low = high_low(jnp.concatenate(left, axis=1))
        twice = mm(jnp.concatenate([a_high, a_low], axis=0), high_ref[depth, :])
        term = twice[:lines] + twice[lines:] + mm(a_high, low_ref[depth, :])
        total = term if total is None else total + term
    out_ref[...] = total * scale_ref[side * lines : (side + 1) * lines, :]


def expand_kernel(side, own_ref, other_ref, rows_ref, vir_ref, *refs):
    out_ref, held, sems = refs[-3:]
    upper = lax.axis_index("yh")
    lane = iota((1, 2 * SLOTS), 1)
    mine = (lane & HALF) == 0
    wanted = rank_of(lane & 15, jnp.where(mine, upper, 1 - upper)).astype(f32)
    sign = jnp.where(mine, 1.0, -1.0)
    vir = flat(vir_ref).astype(f32)
    copies = []
    for r in range(PART):
        slots = slice(r * HALF, (r + 1) * HALF)
        i = side * PART + r
        packed = jnp.concatenate([own_ref[slots, :], other_ref[slots, :]], axis=0)
        high, low = high_low(packed)
        pick = jnp.where(rows_ref[:, BLOCKS + i : BLOCKS + i + 1] == wanted, sign, 0.0).astype(bf16)
        spread = mm(pick, jnp.concatenate([high, low], axis=0))
        spread = jnp.where(rows_ref[:, i : i + 1] == vir, spread, 0.0)
        held[0, r] = spread
        held[1, r] = -spread
        for mirror in range(2):
            copies.append(
                pltpu.make_async_copy(
                    held.at[mirror, r], out_ref.at[mirror, other_block(i)], sems.at[mirror, r]
                )
            )
            copies[-1].start()
    for copy in copies:
        copy.wait()


VMEM = pl.BlockSpec(memory_space=pltpu.VMEM)
SMEM = pl.BlockSpec(memory_space=pltpu.SMEM)
ANY = pl.BlockSpec(memory_space=pl.ANY)
HBM = pl.BlockSpec(memory_space=pltpu.HBM)


SMALL = pl.CostEstimate(flops=1000, bytes_accessed=1000, transcendentals=0)


def params(mib):
    return pltpu.CompilerParams(vmem_limit_bytes=mib * MIB)


def swapped(x, *axes):
    axes = tuple(sorted(axes, key=(ROW + COL).index))
    count = 1 << len(axes)
    return lax.ppermute(x, axes, [(i, count - 1 - i) for i in range(count)])


def one_pass(base, amplitudes, integrals, occ, cd, vir, energy, vir_energy):
    depth, width = integrals.shape
    shape = jax.ShapeDtypeStruct
    token = shape((1, HALF, BLOCK), f32)
    packed = pl.pallas_call(
        pack_kernel,
        out_shape=shape((8, HALF + META, BLOCK), f32),
        in_specs=[SMEM, VMEM, VMEM, VMEM],
        out_specs=VMEM,
        compiler_params=params(8),
    )(base, amplitudes, occ, cd)
    scale, rows, listed, passes = pl.pallas_call(
        table_kernel,
        out_shape=[
            shape((BLOCKS * HALF, width), f32),
            shape((BLOCK, BLOCK), f32),
            token,
            shape((1,), i32),
        ],
        in_specs=[SMEM, VMEM, VMEM, VMEM, VMEM],
        out_specs=[VMEM, VMEM, VMEM, SMEM],
        compiler_params=params(8),
        cost_estimate=SMALL,
    )(base, occ, energy, vir, vir_energy)

    v, loaded = pl.pallas_call(
        load_kernel,
        out_shape=[shape((COLS, BLOCK, width), f32), token],
        in_specs=[HBM],
        out_specs=[VMEM] * 2,
        scratch_shapes=[pltpu.SemaphoreType.DMA((COLS,))],
        compiler_params=params(8),
        cost_estimate=SMALL,
    )(integrals)

    met = lax.all_to_all(packed, NEAR, 0, 0, tiled=True)
    met = met[:4] + met[4:]
    x = met[:, :HALF].reshape(-1, BLOCK)
    meta = (met[:2, HALF:] + met[2:, HALF:]).reshape(-1, BLOCK)
    for step, token_done in zip(COL_STEPS, (loaded, listed, None)):
        there = swapped(jnp.concatenate([x, meta], axis=0), *step)
        meta = meta + there[x.shape[0] :]
        x = jnp.concatenate([x, there[: x.shape[0]]], axis=0)
        if token_done is not None:
            meta = meta + token_done[0]
    x = x.reshape(-1, HALF, BLOCK)
    near = swapped(x, "core")
    high, low, split = pl.pallas_call(
        split_kernel,
        out_shape=[shape((depth, width), bf16), shape((depth, width), bf16), token],
        in_specs=[VMEM] * 3,
        out_specs=[VMEM] * 3,
        compiler_params=params(24),
        cost_estimate=SMALL,
    )(meta, vir, v)

    def ladder(side, near, far, *before):
        return pl.pallas_call(
            functools.partial(ladder_kernel, side),
            out_shape=[shape((PART * HALF, width), f32), token],
            in_specs=[VMEM] * 5 + [ANY] * len(before),
            out_specs=[VMEM] * 2,
            compiler_params=params(24),
            cost_estimate=SMALL,
        )(near, far, high, low, scale, *before)

    def expand(side, own, other, *out):
        return pl.pallas_call(
            functools.partial(expand_kernel, side),
            out_shape=pltpu.HBM((2, BLOCKS, BLOCK, width), f32),
            in_specs=[VMEM] * 4 + [HBM] * len(out),
            out_specs=HBM,
            scratch_shapes=[
                pltpu.VMEM((2, PART, BLOCK, width), f32),
                pltpu.SemaphoreType.DMA((2, PART)),
            ],
            input_output_aliases={4: 0} if out else {},
            compiler_params=params(24),
            cost_estimate=SMALL,
        )(own, other, rows, vir, *out)

    beyond = swapped(x, *X_STEP)
    first, done = ladder(0, x, near)
    first_met = swapped(first, "yh")
    beyond = jnp.concatenate([beyond, done + split], axis=0)
    second, _ = ladder(1, beyond, swapped(beyond, "core"), first_met)
    second_met = swapped(second, "yh")
    out = expand(0, first, first_met)
    out = expand(1, second, second_met, out)
    return out, passes[0]


def local(amplitudes, integrals, occ_irrep, cd_irrep, vir_irrep, occ_energy, vir_energy):
    run = functools.partial(
        one_pass,
        amplitudes=amplitudes,
        integrals=integrals,
        occ=occ_irrep.reshape(-1, BLOCK),
        cd=cd_irrep.reshape(1, -1),
        vir=vir_irrep.reshape(-1, BLOCK),
        energy=occ_energy.reshape(-1, BLOCK),
        vir_energy=vir_energy.reshape(-1, BLOCK),
    )
    out, passes = run(jnp.zeros((1,), i32))

    def more(state):
        return state[0] < passes

    def step(state):
        index, total = state
        extra, _ = run(jnp.full((1,), index, i32))
        return index + 1, total + extra

    _, out = lax.while_loop(more, step, (jnp.int32(1), out))
    return out.reshape(occ_irrep.shape[0], -1)


def solution(mesh):
    bits = Mesh(mesh.devices.reshape((2,) * 8), ROW + COL)
    in_specs = (
        P(ROW, COL),
        P(None, ROW + COL),
        P(),
        P(COL),
        P(ROW + COL),
        P(),
        P(ROW + COL),
    )
    out_specs = P(None, ROW + COL)
    return jax.shard_map(local, mesh=bits, in_specs=in_specs, out_specs=out_specs, check_vma=False)
```

```python
import functools

import jax
import jax.numpy as jnp
from jax import lax
from jax.experimental import pallas as pl
from jax.experimental.pallas import tpu as pltpu
from jax.sharding import Mesh
from jax.sharding import PartitionSpec as P

BLOCK = 128
IRREPS = 8
HALF = 16
META = 8
SLOTS = 2 * HALF
BLOCKS = 8
COLS = 16
PART = BLOCKS // 2
SPLIT = 2

ROW = ("yh", "yl", "xh", "core")
COL = ("xl", "z2", "z1", "z0")

NEAR = ("yh", "yl", "xl")
COL_STEPS = (("z2", "z1"), ("z1",), ("z0",))
X_STEP = ("xh", "xl")

f32, bf16, i32 = jnp.float32, jnp.bfloat16, jnp.int32
MIB = 1 << 20


def iota(shape, dim):
    return lax.broadcasted_iota(i32, shape, dim)


def strict_upper():
    return jnp.where(iota((BLOCK, BLOCK), 0) < iota((BLOCK, BLOCK), 1), 1.0, 0.0).astype(bf16)


def mm(a, b):
    return jnp.dot(a, b, preferred_element_type=f32)


def high_low(x):
    high = x.astype(bf16)
    return high, (x - high.astype(f32)).astype(bf16)


def number(axes):
    total = 0
    for axis in axes:
        total = 2 * total + lax.axis_index(axis)
    return total


def own_block():
    return number(ROW[1:])


def other_block(index):
    xh = lax.axis_index("xh") ^ (index >> 2)
    core = lax.axis_index("core") ^ (index >> 1 & 1)
    return (index & 1) * 4 + xh * 2 + core


def other_col(index):
    mask = 0
    for place, step in enumerate(COL_STEPS):
        if index >> 1 + place & 1:
            mask ^= sum(1 << (len(COL) - 1 - COL.index(axis)) for axis in step)
    return (index & 1) * 8 + (number(COL[1:]) ^ mask)


def rank_of(slot, upper):
    return 2 * slot + upper


def flat(ref):
    return jnp.concatenate([ref[i : i + 1, :] for i in range(ref.shape[0])], axis=1)


def pack_kernel(base_ref, amp_ref, occ_ref, cd_ref, out_ref):
    upper = lax.axis_index("yh")
    y = number(("yh", "yl"))
    occ = occ_ref[pl.ds(own_block(), 1), :]
    same = jnp.where(occ == iota((IRREPS, BLOCK), 0), 1.0, 0.0)
    ranks = mm(same.astype(bf16), strict_upper())
    rank = jnp.sum(same * ranks, axis=0, keepdims=True).astype(i32)
    key = occ * BLOCK + rank - base_ref[0] * SLOTS
    line = iota((2 * BLOCK, BLOCK), 0)
    wanted = ((line >> 4) & 7) * BLOCK + rank_of(line & 15, line >> 7)
    pick = jnp.where(key == wanted, 1.0, 0.0).astype(bf16)
    amp = amp_ref[...]
    first = amp.astype(bf16)
    rest = amp - first.astype(f32)
    second = rest.astype(bf16)
    third = (rest - second.astype(f32)).astype(bf16)
    packed = mm(pick, first) + mm(pick, second) + mm(pick, third)
    cd = cd_ref[...]
    sign = (1 - 2 * upper).astype(f32)
    tile = jnp.where(iota((META, BLOCK), 0) == number(COL[1:]), cd.astype(f32), 0.0)
    for side in range(2):
        total = jnp.zeros((HALF, BLOCK), f32)
        for g in range(IRREPS):
            lines = packed[side * BLOCK + g * HALF : side * BLOCK + (g + 1) * HALF]
            total = total + jnp.where(cd == g, lines, 0.0)
        total = sign * total
        for yl in range(2):
            mine = jnp.where(y == 2 * side + yl, tile, 0.0)
            for xl in range(2):
                place = 4 * side + 2 * yl + xl
                out_ref[place, :HALF, :] = total
                out_ref[place, HALF:, :] = mine


def table_kernel(
    base_ref, occ_ref, energy_ref, vir_ref, vir_energy_ref, scale_ref, rows_ref, token_ref, passes_ref
):
    token_ref[...] = jnp.zeros(token_ref.shape, f32)
    upper = lax.axis_index("yh")

    def ordered(ref):
        return jnp.concatenate(
            [ref[pl.ds(other_block(i), 1), :] for i in range(BLOCKS)], axis=0
        )

    occ = ordered(occ_ref)
    energy = ordered(energy_ref)
    irrep = iota((IRREPS, BLOCK), 0)
    same = jnp.concatenate(
        [jnp.where(occ[b : b + 1] == irrep, 1.0, 0.0) for b in range(BLOCKS)], axis=0
    )
    ranks = mm(same.astype(bf16), strict_upper())
    counts = jnp.sum(same, axis=1, keepdims=True)
    most = jnp.max(counts).astype(i32)
    passes_ref[0] = (most + SLOTS - 1) // SLOTS
    rank = jnp.concatenate(
        [
            jnp.sum((same * ranks)[b * IRREPS : (b + 1) * IRREPS], axis=0, keepdims=True)
            for b in range(BLOCKS)
        ],
        axis=0,
    ).astype(i32) - base_ref[0] * SLOTS
    both = jnp.concatenate(
        [occ.astype(f32), rank.astype(f32), jnp.zeros((BLOCK - 2 * BLOCKS, BLOCK), f32)], axis=0
    )
    rows_ref[...] = both.T
    key = occ * BLOCK + rank
    line = iota((BLOCK, BLOCK), 0)
    wanted = (line >> 4) * BLOCK + rank_of(line & 15, upper)
    vir = flat(vir_ref)
    vir_energy = flat(vir_energy_ref)
    for b in range(BLOCKS):
        found = jnp.sum(
            jnp.where(key[b : b + 1] == wanted, energy[b : b + 1], 0.0), axis=1, keepdims=True
        )
        at_slot = jnp.zeros((HALF, vir.shape[1]), f32)
        for g in range(IRREPS):
            at_slot = at_slot + jnp.where(vir == g, found[g * HALF : (g + 1) * HALF], 0.0)
        scale_ref[b * HALF : (b + 1) * HALF, :] = 0.5 / (at_slot - vir_energy)


def load_kernel(v_ref, out_ref, token_ref, sems):
    token_ref[...] = jnp.zeros(token_ref.shape, f32)
    copies = []
    for j in range(COLS):
        start = pl.multiple_of(other_col(j) * BLOCK, BLOCK)
        copies.append(pltpu.make_async_copy(v_ref.at[pl.ds(start, BLOCK)], out_ref.at[j], sems.at[j]))
        copies[-1].start()
    for copy in copies:
        copy.wait()


def split_kernel(meta_ref, vir_ref, held_ref, high_ref, low_ref, token_ref):
    token_ref[...] = jnp.zeros(token_ref.shape, f32)
    meta = jnp.concatenate(
        [meta_ref[pl.ds(other_col(j), 1), :] for j in range(COLS)]
        + [jnp.zeros((BLOCK - COLS, BLOCK), f32)],
        axis=0,
    ).T
    vir = flat(vir_ref).astype(f32)
    for j in range(COLS):
        high, low = high_low(jnp.where(meta[:, j : j + 1] == vir, held_ref[j], 0.0))
        high_ref[j * BLOCK : (j + 1) * BLOCK, :] = high
        low_ref[j * BLOCK : (j + 1) * BLOCK, :] = low


def places(j):
    return [(j >> 1) * 4 + 2 * yl + (j & 1) for yl in range(2)]


def ladder_kernel(side, near_ref, *refs):
    far_refs, (high_ref, low_ref, scale_ref, out_ref), token_ref = refs[:SPLIT], refs[SPLIT : SPLIT + 4], refs[SPLIT + 4 :]
    step = 2 * COLS // SPLIT
    for ref in token_ref:
        ref[...] = jnp.zeros(ref.shape, f32)
    lines = PART * HALF
    total = None
    group = 4
    for j0 in range(0, COLS, group):
        left = [
            jnp.concatenate(
                [near_ref[e] for e in places(j)]
                + [far_refs[e // step][e % step] for e in places(j)],
                axis=0,
            )
            for j in range(j0, j0 + group)
        ]
        depth = slice(j0 * BLOCK, (j0 + group) * BLOCK)
        a_high, a_low = high_low(jnp.concatenate(left, axis=1))
        twice = mm(jnp.concatenate([a_high, a_low], axis=0), high_ref[depth, :])
        term = twice[:lines] + twice[lines:] + mm(a_high, low_ref[depth, :])
        total = term if total is None else total + term
    out_ref[...] = total * scale_ref[side * lines : (side + 1) * lines, :]


def expand_kernel(side, own_ref, other_ref, rows_ref, vir_ref, *refs):
    out_ref, held, sems = refs[-3:]
    upper = lax.axis_index("yh")
    lane = iota((1, 2 * SLOTS), 1)
    mine = (lane & HALF) == 0
    wanted = rank_of(lane & 15, jnp.where(mine, upper, 1 - upper)).astype(f32)
    sign = jnp.where(mine, 1.0, -1.0)
    vir = flat(vir_ref).astype(f32)
    copies = []
    for r in range(PART):
        slots = slice(r * HALF, (r + 1) * HALF)
        i = side * PART + r
        packed = jnp.concatenate([own_ref[slots, :], other_ref[slots, :]], axis=0)
        high, low = high_low(packed)
        pick = jnp.where(rows_ref[:, BLOCKS + i : BLOCKS + i + 1] == wanted, sign, 0.0).astype(bf16)
        spread = mm(pick, jnp.concatenate([high, low], axis=0))
        spread = jnp.where(rows_ref[:, i : i + 1] == vir, spread, 0.0)
        held[0, r] = spread
        held[1, r] = -spread
        for mirror in range(2):
            copies.append(
                pltpu.make_async_copy(
                    held.at[mirror, r], out_ref.at[mirror, other_block(i)], sems.at[mirror, r]
                )
            )
            copies[-1].start()
    for copy in copies:
        copy.wait()


VMEM = pl.BlockSpec(memory_space=pltpu.VMEM)
SMEM = pl.BlockSpec(memory_space=pltpu.SMEM)
ANY = pl.BlockSpec(memory_space=pl.ANY)
HBM = pl.BlockSpec(memory_space=pltpu.HBM)


SMALL = pl.CostEstimate(flops=1000, bytes_accessed=1000, transcendentals=0)


def params(mib):
    return pltpu.CompilerParams(vmem_limit_bytes=mib * MIB)


def swapped(x, *axes):
    axes = tuple(sorted(axes, key=(ROW + COL).index))
    count = 1 << len(axes)
    return lax.ppermute(x, axes, [(i, count - 1 - i) for i in range(count)])


def core_swapped(x, token=None):
    parts = jnp.split(x, SPLIT)
    if token is not None:
        parts = [jnp.concatenate([part, token], axis=0) for part in parts]
    return [swapped(part, "core") for part in parts]


def one_pass(base, amplitudes, integrals, occ, cd, vir, energy, vir_energy):
    depth, width = integrals.shape
    shape = jax.ShapeDtypeStruct
    token = shape((1, HALF, BLOCK), f32)
    packed = pl.pallas_call(
        pack_kernel,
        out_shape=shape((8, HALF + META, BLOCK), f32),
        in_specs=[SMEM, VMEM, VMEM, VMEM],
        out_specs=VMEM,
        compiler_params=params(8),
    )(base, amplitudes, occ, cd)
    scale, rows, listed, passes = pl.pallas_call(
        table_kernel,
        out_shape=[
            shape((BLOCKS * HALF, width), f32),
            shape((BLOCK, BLOCK), f32),
            token,
            shape((1,), i32),
        ],
        in_specs=[SMEM, VMEM, VMEM, VMEM, VMEM],
        out_specs=[VMEM, VMEM, VMEM, SMEM],
        compiler_params=params(8),
        cost_estimate=SMALL,
    )(base, occ, energy, vir, vir_energy)

    v, loaded = pl.pallas_call(
        load_kernel,
        out_shape=[shape((COLS, BLOCK, width), f32), token],
        in_specs=[HBM],
        out_specs=[VMEM] * 2,
        scratch_shapes=[pltpu.SemaphoreType.DMA((COLS,))],
        compiler_params=params(8),
        cost_estimate=SMALL,
    )(integrals)

    met = lax.all_to_all(packed, NEAR, 0, 0, tiled=True)
    met = met[:4] + met[4:]
    x = met[:, :HALF].reshape(-1, BLOCK)
    meta = (met[:2, HALF:] + met[2:, HALF:]).reshape(-1, BLOCK)
    for step, token_done in zip(COL_STEPS, (loaded, listed, None)):
        there = swapped(jnp.concatenate([x, meta], axis=0), *step)
        meta = meta + there[x.shape[0] :]
        x = jnp.concatenate([x, there[: x.shape[0]]], axis=0)
        if token_done is not None:
            meta = meta + token_done[0]
    x = x.reshape(-1, HALF, BLOCK)
    beyond = swapped(x, *X_STEP)
    near = core_swapped(x)
    high, low, split = pl.pallas_call(
        split_kernel,
        out_shape=[shape((depth, width), bf16), shape((depth, width), bf16), token],
        in_specs=[VMEM] * 3,
        out_specs=[VMEM] * 3,
        compiler_params=params(24),
        cost_estimate=SMALL,
    )(meta, vir, v)

    def ladder(side, near, far):
        return pl.pallas_call(
            functools.partial(ladder_kernel, side),
            out_shape=[shape((PART * HALF, width), f32)] + [token] * (1 - side),
            in_specs=[VMEM] * (4 + SPLIT),
            out_specs=[VMEM] * (2 - side),
            compiler_params=params(24),
            cost_estimate=SMALL,
        )(near, *far, high, low, scale)

    def expand(side, own, other, *out):
        return pl.pallas_call(
            functools.partial(expand_kernel, side),
            out_shape=pltpu.HBM((2, BLOCKS, BLOCK, width), f32),
            in_specs=[VMEM] * 4 + [HBM] * len(out),
            out_specs=HBM,
            scratch_shapes=[
                pltpu.VMEM((2, PART, BLOCK, width), f32),
                pltpu.SemaphoreType.DMA((2, PART)),
            ],
            input_output_aliases={4: 0} if out else {},
            compiler_params=params(24),
            cost_estimate=SMALL,
        )(own, other, rows, vir, *out)

    first, done = ladder(0, x, near)
    first_met = swapped(first, "yh")
    (second,) = ladder(1, beyond, core_swapped(beyond, done + split))
    second_met = swapped(second, "yh")
    out = expand(0, first, first_met)
    out = expand(1, second, second_met, out)
    return out, passes[0]


def local(amplitudes, integrals, occ_irrep, cd_irrep, vir_irrep, occ_energy, vir_energy):
    run = functools.partial(
        one_pass,
        amplitudes=amplitudes,
        integrals=integrals,
        occ=occ_irrep.reshape(-1, BLOCK),
        cd=cd_irrep.reshape(1, -1),
        vir=vir_irrep.reshape(-1, BLOCK),
        energy=occ_energy.reshape(-1, BLOCK),
        vir_energy=vir_energy.reshape(-1, BLOCK),
    )
    out, passes = run(jnp.zeros((1,), i32))

    def more(state):
        return state[0] < passes

    def step(state):
        index, total = state
        extra, _ = run(jnp.full((1,), index, i32))
        return index + 1, total + extra

    _, out = lax.while_loop(more, step, (jnp.int32(1), out))
    return out.reshape(occ_irrep.shape[0], -1)


def solution(mesh):
    bits = Mesh(mesh.devices.reshape((2,) * 8), ROW + COL)
    in_specs = (
        P(ROW, COL),
        P(None, ROW + COL),
        P(),
        P(COL),
        P(ROW + COL),
        P(),
        P(ROW + COL),
    )
    out_specs = P(None, ROW + COL)
    return jax.shard_map(local, mesh=bits, in_specs=in_specs, out_specs=out_specs, check_vma=False)
```

```python
import functools

import jax
import jax.numpy as jnp
from jax import lax
from jax.experimental import pallas as pl
from jax.experimental.pallas import tpu as pltpu
from jax.sharding import Mesh
from jax.sharding import PartitionSpec as P

BLOCK = 128
IRREPS = 8
HALF = 16
META = 8
SLOTS = 2 * HALF
BLOCKS = 8
COLS = 16
PART = BLOCKS // 2
SPLIT = 2

ROW = ("yh", "yl", "xh", "core")
COL = ("xl", "z2", "z1", "z0")

NEAR = ("yh", "yl", "xl")
COL_STEPS = (("z2", "z1"), ("z1",), ("z0",))
X_STEP = ("xh", "xl")

f32, bf16, i32 = jnp.float32, jnp.bfloat16, jnp.int32
MIB = 1 << 20


def iota(shape, dim):
    return lax.broadcasted_iota(i32, shape, dim)


def strict_upper():
    return jnp.where(iota((BLOCK, BLOCK), 0) < iota((BLOCK, BLOCK), 1), 1.0, 0.0).astype(bf16)


def mm(a, b):
    return jnp.dot(a, b, preferred_element_type=f32)


def high_low(x):
    high = x.astype(bf16)
    return high, (x - high.astype(f32)).astype(bf16)


def number(axes):
    total = 0
    for axis in axes:
        total = 2 * total + lax.axis_index(axis)
    return total


def own_block():
    return number(ROW[1:])


def other_block(index):
    xh = lax.axis_index("xh") ^ (index >> 2)
    core = lax.axis_index("core") ^ (index >> 1 & 1)
    return (index & 1) * 4 + xh * 2 + core


def other_col(index):
    mask = 0
    for place, step in enumerate(COL_STEPS):
        if index >> 1 + place & 1:
            mask ^= sum(1 << (len(COL) - 1 - COL.index(axis)) for axis in step)
    return (index & 1) * 8 + (number(COL[1:]) ^ mask)


def rank_of(slot, upper):
    return 2 * slot + upper


def flat(ref):
    return jnp.concatenate([ref[i : i + 1, :] for i in range(ref.shape[0])], axis=1)


def pack_kernel(base_ref, amp_ref, occ_ref, cd_ref, out_ref):
    upper = lax.axis_index("yh")
    y = number(("yh", "yl"))
    occ = occ_ref[pl.ds(own_block(), 1), :]
    same = jnp.where(occ == iota((IRREPS, BLOCK), 0), 1.0, 0.0)
    ranks = mm(same.astype(bf16), strict_upper())
    rank = jnp.sum(same * ranks, axis=0, keepdims=True).astype(i32)
    key = occ * BLOCK + rank - base_ref[0] * SLOTS
    line = iota((2 * BLOCK, BLOCK), 0)
    wanted = ((line >> 4) & 7) * BLOCK + rank_of(line & 15, line >> 7)
    pick = jnp.where(key == wanted, 1.0, 0.0).astype(bf16)
    amp = amp_ref[...]
    first = amp.astype(bf16)
    rest = amp - first.astype(f32)
    second = rest.astype(bf16)
    third = (rest - second.astype(f32)).astype(bf16)
    packed = mm(pick, first) + mm(pick, second) + mm(pick, third)
    cd = cd_ref[...]
    sign = (1 - 2 * upper).astype(f32)
    tile = jnp.where(iota((META, BLOCK), 0) == number(COL[1:]), cd.astype(f32), 0.0)
    for side in range(2):
        total = jnp.zeros((HALF, BLOCK), f32)
        for g in range(IRREPS):
            lines = packed[side * BLOCK + g * HALF : side * BLOCK + (g + 1) * HALF]
            total = total + jnp.where(cd == g, lines, 0.0)
        total = sign * total
        for yl in range(2):
            mine = jnp.where(y == 2 * side + yl, tile, 0.0)
            for xl in range(2):
                place = 4 * side + 2 * yl + xl
                out_ref[place, :HALF, :] = total
                out_ref[place, HALF:, :] = mine


def table_kernel(
    base_ref, occ_ref, energy_ref, vir_ref, vir_energy_ref, scale_ref, rows_ref, token_ref, passes_ref
):
    token_ref[...] = jnp.zeros(token_ref.shape, f32)
    upper = lax.axis_index("yh")

    def ordered(ref):
        return jnp.concatenate(
            [ref[pl.ds(other_block(i), 1), :] for i in range(BLOCKS)], axis=0
        )

    occ = ordered(occ_ref)
    energy = ordered(energy_ref)
    irrep = iota((IRREPS, BLOCK), 0)
    same = jnp.concatenate(
        [jnp.where(occ[b : b + 1] == irrep, 1.0, 0.0) for b in range(BLOCKS)], axis=0
    )
    ranks = mm(same.astype(bf16), strict_upper())
    counts = jnp.sum(same, axis=1, keepdims=True)
    most = jnp.max(counts).astype(i32)
    passes_ref[0] = (most + SLOTS - 1) // SLOTS
    rank = jnp.concatenate(
        [
            jnp.sum((same * ranks)[b * IRREPS : (b + 1) * IRREPS], axis=0, keepdims=True)
            for b in range(BLOCKS)
        ],
        axis=0,
    ).astype(i32) - base_ref[0] * SLOTS
    both = jnp.concatenate(
        [occ.astype(f32), rank.astype(f32), jnp.zeros((BLOCK - 2 * BLOCKS, BLOCK), f32)], axis=0
    )
    rows_ref[...] = both.T
    key = occ * BLOCK + rank
    line = iota((BLOCK, BLOCK), 0)
    wanted = (line >> 4) * BLOCK + rank_of(line & 15, upper)
    vir = flat(vir_ref)
    vir_energy = flat(vir_energy_ref)
    for b in range(BLOCKS):
        found = jnp.sum(
            jnp.where(key[b : b + 1] == wanted, energy[b : b + 1], 0.0), axis=1, keepdims=True
        )
        at_slot = jnp.zeros((HALF, vir.shape[1]), f32)
        for g in range(IRREPS):
            at_slot = at_slot + jnp.where(vir == g, found[g * HALF : (g + 1) * HALF], 0.0)
        scale_ref[b * HALF : (b + 1) * HALF, :] = 0.5 / (at_slot - vir_energy)


def load_kernel(v_ref, out_ref, token_ref, sems):
    token_ref[...] = jnp.zeros(token_ref.shape, f32)
    copies = []
    for j in range(COLS):
        start = pl.multiple_of(other_col(j) * BLOCK, BLOCK)
        copies.append(pltpu.make_async_copy(v_ref.at[pl.ds(start, BLOCK)], out_ref.at[j], sems.at[j]))
        copies[-1].start()
    for copy in copies:
        copy.wait()


def split_kernel(part, meta_ref, vir_ref, held_ref, high_ref, low_ref, token_ref):
    token_ref[...] = jnp.zeros(token_ref.shape, f32)
    columns = range(part * (COLS // 2), (part + 1) * (COLS // 2))
    meta = jnp.concatenate(
        [meta_ref[pl.ds(other_col(j), 1), :] for j in columns]
        + [jnp.zeros((BLOCK - COLS // 2, BLOCK), f32)],
        axis=0,
    ).T
    vir = flat(vir_ref).astype(f32)
    for place, j in enumerate(columns):
        high, low = high_low(jnp.where(meta[:, place : place + 1] == vir, held_ref[j], 0.0))
        high_ref[place * BLOCK : (place + 1) * BLOCK, :] = high
        low_ref[place * BLOCK : (place + 1) * BLOCK, :] = low


def places(j):
    return [(j >> 1) * 4 + 2 * yl + (j & 1) for yl in range(2)]


def ladder_kernel(side, near_ref, *refs):
    far_refs, (high_refs, low_refs) = refs[:SPLIT], (refs[SPLIT : SPLIT + 4 : 2], refs[SPLIT + 1 : SPLIT + 4 : 2])
    scale_ref, out_ref, *token_ref = refs[SPLIT + 4 :]
    step = 2 * COLS // SPLIT
    for ref in token_ref:
        ref[...] = jnp.zeros(ref.shape, f32)
    lines = PART * HALF
    total = None
    group = 4
    for j0 in range(0, COLS, group):
        left = [
            jnp.concatenate(
                [near_ref[e] for e in places(j)]
                + [far_refs[e // step][e % step] for e in places(j)],
                axis=0,
            )
            for j in range(j0, j0 + group)
        ]
        part, first = divmod(j0, COLS // 2)
        depth = slice(first * BLOCK, (first + group) * BLOCK)
        a_high, a_low = high_low(jnp.concatenate(left, axis=1))
        twice = mm(jnp.concatenate([a_high, a_low], axis=0), high_refs[part][depth, :])
        term = twice[:lines] + twice[lines:] + mm(a_high, low_refs[part][depth, :])
        total = term if total is None else total + term
    out_ref[...] = total * scale_ref[side * lines : (side + 1) * lines, :]


def expand_kernel(side, own_ref, other_ref, rows_ref, vir_ref, *refs):
    out_ref, held, sems = refs[-3:]
    upper = lax.axis_index("yh")
    lane = iota((1, 2 * SLOTS), 1)
    mine = (lane & HALF) == 0
    wanted = rank_of(lane & 15, jnp.where(mine, upper, 1 - upper)).astype(f32)
    sign = jnp.where(mine, 1.0, -1.0)
    vir = flat(vir_ref).astype(f32)
    copies = []
    for r in range(PART):
        slots = slice(r * HALF, (r + 1) * HALF)
        i = side * PART + r
        packed = jnp.concatenate([own_ref[slots, :], other_ref[slots, :]], axis=0)
        high, low = high_low(packed)
        pick = jnp.where(rows_ref[:, BLOCKS + i : BLOCKS + i + 1] == wanted, sign, 0.0).astype(bf16)
        spread = mm(pick, jnp.concatenate([high, low], axis=0))
        spread = jnp.where(rows_ref[:, i : i + 1] == vir, spread, 0.0)
        held[0, r] = spread
        held[1, r] = -spread
        for mirror in range(2):
            copies.append(
                pltpu.make_async_copy(
                    held.at[mirror, r], out_ref.at[mirror, other_block(i)], sems.at[mirror, r]
                )
            )
            copies[-1].start()
    for copy in copies:
        copy.wait()


def join_kernel(in_ref, after_ref, out_ref):
    pass


VMEM = pl.BlockSpec(memory_space=pltpu.VMEM)
SMEM = pl.BlockSpec(memory_space=pltpu.SMEM)
ANY = pl.BlockSpec(memory_space=pl.ANY)
HBM = pl.BlockSpec(memory_space=pltpu.HBM)


SMALL = pl.CostEstimate(flops=1000, bytes_accessed=1000, transcendentals=0)


def params(mib):
    return pltpu.CompilerParams(vmem_limit_bytes=mib * MIB)


def swapped(x, *axes):
    axes = tuple(sorted(axes, key=(ROW + COL).index))
    count = 1 << len(axes)
    return lax.ppermute(x, axes, [(i, count - 1 - i) for i in range(count)])


def core_swapped(x, token=None):
    parts = jnp.split(x, SPLIT)
    if token is not None:
        parts = [jnp.concatenate([part, token], axis=0) for part in parts]
    return [swapped(part, "core") for part in parts]


def one_pass(base, amplitudes, integrals, occ, cd, vir, energy, vir_energy):
    depth, width = integrals.shape
    shape = jax.ShapeDtypeStruct
    token = shape((1, HALF, BLOCK), f32)
    packed = pl.pallas_call(
        pack_kernel,
        out_shape=shape((8, HALF + META, BLOCK), f32),
        in_specs=[SMEM, VMEM, VMEM, VMEM],
        out_specs=VMEM,
        compiler_params=params(8),
    )(base, amplitudes, occ, cd)
    scale, rows, listed, passes = pl.pallas_call(
        table_kernel,
        out_shape=[
            shape((BLOCKS * HALF, width), f32),
            shape((BLOCK, BLOCK), f32),
            token,
            shape((1,), i32),
        ],
        in_specs=[SMEM, VMEM, VMEM, VMEM, VMEM],
        out_specs=[VMEM, VMEM, VMEM, SMEM],
        compiler_params=params(8),
        cost_estimate=SMALL,
    )(base, occ, energy, vir, vir_energy)

    v, loaded = pl.pallas_call(
        load_kernel,
        out_shape=[shape((COLS, BLOCK, width), f32), token],
        in_specs=[HBM],
        out_specs=[VMEM] * 2,
        scratch_shapes=[pltpu.SemaphoreType.DMA((COLS,))],
        compiler_params=params(8),
        cost_estimate=SMALL,
    )(integrals)

    met = lax.all_to_all(packed, NEAR, 0, 0, tiled=True)
    met = met[:4] + met[4:]
    x = met[:, :HALF].reshape(-1, BLOCK)
    meta = (met[:2, HALF:] + met[2:, HALF:]).reshape(-1, BLOCK)
    def split(part, meta):
        return pl.pallas_call(
            functools.partial(split_kernel, part),
            out_shape=[shape((depth // 2, width), bf16), shape((depth // 2, width), bf16), token],
            in_specs=[VMEM] * 3,
            out_specs=[VMEM] * 3,
            compiler_params=params(24),
            cost_estimate=SMALL,
        )(meta, vir, v)

    for step, token_done in zip(COL_STEPS, (listed, loaded, None)):
        there = swapped(jnp.concatenate([x, meta], axis=0), *step)
        meta = meta + there[x.shape[0] :]
        x = jnp.concatenate([x, there[: x.shape[0]]], axis=0)
        if token_done is not None:
            known = meta
            meta = meta + token_done[0]
    x = x.reshape(-1, HALF, BLOCK)
    *early, early_token = split(0, known)
    beyond = swapped(jnp.concatenate([x, early_token], axis=0), *X_STEP)[:-1]
    near = core_swapped(x)
    *late, late_token = split(1, meta)

    def ladder(side, near, far):
        return pl.pallas_call(
            functools.partial(ladder_kernel, side),
            out_shape=[shape((PART * HALF, width), f32)] + [token] * (1 - side),
            in_specs=[VMEM] * (6 + SPLIT),
            out_specs=[VMEM] * (2 - side),
            compiler_params=params(24),
            cost_estimate=SMALL,
        )(near, *far, *early, *late, scale)

    def expand(side, own, other, *out):
        return pl.pallas_call(
            functools.partial(expand_kernel, side),
            out_shape=pltpu.HBM((2, BLOCKS, BLOCK, width), f32),
            in_specs=[VMEM] * 4 + [HBM] * len(out),
            out_specs=HBM,
            scratch_shapes=[
                pltpu.VMEM((2, PART, BLOCK, width), f32),
                pltpu.SemaphoreType.DMA((2, PART)),
            ],
            input_output_aliases={4: 0} if out else {},
            compiler_params=params(24),
            cost_estimate=SMALL,
        )(own, other, rows, vir, *out)

    first, done = ladder(0, x, near)
    first_met = swapped(first, "yh")
    (second,) = ladder(1, beyond, core_swapped(beyond, done + late_token))
    second = pl.pallas_call(
        join_kernel,
        out_shape=shape(second.shape, f32),
        in_specs=[ANY, ANY],
        out_specs=ANY,
        input_output_aliases={0: 0},
        compiler_params=params(8),
        cost_estimate=SMALL,
    )(second, first_met)
    second_met = swapped(second, "yh")
    out = expand(0, first, first_met)
    out = expand(1, second, second_met, out)
    return out, passes[0]


def local(amplitudes, integrals, occ_irrep, cd_irrep, vir_irrep, occ_energy, vir_energy):
    run = functools.partial(
        one_pass,
        amplitudes=amplitudes,
        integrals=integrals,
        occ=occ_irrep.reshape(-1, BLOCK),
        cd=cd_irrep.reshape(1, -1),
        vir=vir_irrep.reshape(-1, BLOCK),
        energy=occ_energy.reshape(-1, BLOCK),
        vir_energy=vir_energy.reshape(-1, BLOCK),
    )
    out, passes = run(jnp.zeros((1,), i32))

    def step(state):
        index, total = state
        extra, _ = run(jnp.full((1,), index, i32))
        return index + 1, total + extra

    def further(total):
        return lax.while_loop(lambda state: state[0] < passes, step, (jnp.int32(1), total))[1]

    out = lax.cond(passes > 1, further, lambda total: total, out)
    return out.reshape(occ_irrep.shape[0], -1)


def solution(mesh):
    bits = Mesh(mesh.devices.reshape((2,) * 8), ROW + COL)
    in_specs = (
        P(ROW, COL),
        P(None, ROW + COL),
        P(),
        P(COL),
        P(ROW + COL),
        P(),
        P(ROW + COL),
    )
    out_specs = P(None, ROW + COL)
    return jax.shard_map(local, mesh=bits, in_specs=in_specs, out_specs=out_specs, check_vma=False)
```

```python
import functools

import jax
import jax.numpy as jnp
from jax import lax
from jax.experimental import pallas as pl
from jax.experimental.pallas import tpu as pltpu
from jax.sharding import Mesh
from jax.sharding import PartitionSpec as P

BLOCK = 128
IRREPS = 8
HALF = 16
META = 8
SLOTS = 2 * HALF
BLOCKS = 8
COLS = 16
PART = BLOCKS // 2
SPLIT = 2

ROW = ("yh", "yl", "xh", "core")
COL = ("xl", "z2", "z1", "z0")

NEAR = ("yh", "yl", "xl")
COL_STEPS = (("z2", "z1"), ("z1",), ("z0",))
X_STEP = ("xh", "xl")

f32, bf16, i32 = jnp.float32, jnp.bfloat16, jnp.int32
MIB = 1 << 20


def iota(shape, dim):
    return lax.broadcasted_iota(i32, shape, dim)


def strict_upper():
    return jnp.where(iota((BLOCK, BLOCK), 0) < iota((BLOCK, BLOCK), 1), 1.0, 0.0).astype(bf16)


def mm(a, b):
    return jnp.dot(a, b, preferred_element_type=f32)


def high_low(x):
    high = x.astype(bf16)
    return high, (x - high.astype(f32)).astype(bf16)


def number(axes):
    total = 0
    for axis in axes:
        total = 2 * total + lax.axis_index(axis)
    return total


def own_block():
    return number(ROW[1:])


def other_block(index):
    xh = lax.axis_index("xh") ^ (index >> 2)
    core = lax.axis_index("core") ^ (index >> 1 & 1)
    return (index & 1) * 4 + xh * 2 + core


def other_col(index):
    mask = 0
    for place, step in enumerate(COL_STEPS):
        if index >> 1 + place & 1:
            mask ^= sum(1 << (len(COL) - 1 - COL.index(axis)) for axis in step)
    return (index & 1) * 8 + (number(COL[1:]) ^ mask)


def rank_of(slot, upper):
    return 2 * slot + upper


def flat(ref):
    return jnp.concatenate([ref[i : i + 1, :] for i in range(ref.shape[0])], axis=1)


def pack_kernel(base_ref, amp_ref, occ_ref, cd_ref, out_ref):
    upper = lax.axis_index("yh")
    y = number(("yh", "yl"))
    occ = occ_ref[pl.ds(own_block(), 1), :]
    same = jnp.where(occ == iota((IRREPS, BLOCK), 0), 1.0, 0.0)
    ranks = mm(same.astype(bf16), strict_upper())
    rank = jnp.sum(same * ranks, axis=0, keepdims=True).astype(i32)
    key = occ * BLOCK + rank - base_ref[0] * SLOTS
    line = iota((2 * BLOCK, BLOCK), 0)
    wanted = ((line >> 4) & 7) * BLOCK + rank_of(line & 15, line >> 7)
    pick = jnp.where(key == wanted, 1.0, 0.0).astype(bf16)
    amp = amp_ref[...]
    first = amp.astype(bf16)
    rest = amp - first.astype(f32)
    second = rest.astype(bf16)
    packed = mm(pick, first) + mm(pick, second)
    cd = cd_ref[...]
    sign = (1 - 2 * upper).astype(f32)
    tile = jnp.where(iota((META, BLOCK), 0) == number(COL[1:]), cd.astype(f32), 0.0)
    for side in range(2):
        total = jnp.zeros((HALF, BLOCK), f32)
        for g in range(IRREPS):
            lines = packed[side * BLOCK + g * HALF : side * BLOCK + (g + 1) * HALF]
            total = total + jnp.where(cd == g, lines, 0.0)
        total = sign * total
        for yl in range(2):
            mine = jnp.where(y == 2 * side + yl, tile, 0.0)
            for xl in range(2):
                place = 4 * side + 2 * yl + xl
                out_ref[place, :HALF, :] = total
                out_ref[place, HALF:, :] = mine


def table_kernel(
    base_ref, occ_ref, energy_ref, vir_ref, vir_energy_ref, scale_ref, rows_ref, token_ref, passes_ref
):
    token_ref[...] = jnp.zeros(token_ref.shape, f32)
    upper = lax.axis_index("yh")

    def ordered(ref):
        return jnp.concatenate(
            [ref[pl.ds(other_block(i), 1), :] for i in range(BLOCKS)], axis=0
        )

    occ = ordered(occ_ref)
    energy = ordered(energy_ref)
    irrep = iota((IRREPS, BLOCK), 0)
    same = jnp.concatenate(
        [jnp.where(occ[b : b + 1] == irrep, 1.0, 0.0) for b in range(BLOCKS)], axis=0
    )
    ranks = mm(same.astype(bf16), strict_upper())
    counts = jnp.sum(same, axis=1, keepdims=True)
    most = jnp.max(counts).astype(i32)
    passes_ref[0] = (most + SLOTS - 1) // SLOTS
    rank = jnp.concatenate(
        [
            jnp.sum((same * ranks)[b * IRREPS : (b + 1) * IRREPS], axis=0, keepdims=True)
            for b in range(BLOCKS)
        ],
        axis=0,
    ).astype(i32) - base_ref[0] * SLOTS
    both = jnp.concatenate(
        [occ.astype(f32), rank.astype(f32), jnp.zeros((BLOCK - 2 * BLOCKS, BLOCK), f32)], axis=0
    )
    rows_ref[...] = both.T
    key = occ * BLOCK + rank
    line = iota((BLOCK, BLOCK), 0)
    wanted = (line >> 4) * BLOCK + rank_of(line & 15, upper)
    vir = flat(vir_ref)
    vir_energy = flat(vir_energy_ref)
    for b in range(BLOCKS):
        found = jnp.sum(
            jnp.where(key[b : b + 1] == wanted, energy[b : b + 1], 0.0), axis=1, keepdims=True
        )
        at_slot = jnp.zeros((HALF, vir.shape[1]), f32)
        for g in range(IRREPS):
            at_slot = at_slot + jnp.where(vir == g, found[g * HALF : (g + 1) * HALF], 0.0)
        scale_ref[b * HALF : (b + 1) * HALF, :] = 0.5 / (at_slot - vir_energy)


def load_kernel(v_ref, out_ref, token_ref, sems):
    token_ref[...] = jnp.zeros(token_ref.shape, f32)
    copies = []
    for j in range(COLS):
        start = pl.multiple_of(other_col(j) * BLOCK, BLOCK)
        copies.append(pltpu.make_async_copy(v_ref.at[pl.ds(start, BLOCK)], out_ref.at[j], sems.at[j]))
        copies[-1].start()
    for copy in copies:
        copy.wait()


def split_kernel(part, meta_ref, vir_ref, held_ref, high_ref, low_ref, token_ref):
    token_ref[...] = jnp.zeros(token_ref.shape, f32)
    columns = range(part * (COLS // 2), (part + 1) * (COLS // 2))
    meta = jnp.concatenate(
        [meta_ref[pl.ds(other_col(j), 1), :] for j in columns]
        + [jnp.zeros((BLOCK - COLS // 2, BLOCK), f32)],
        axis=0,
    ).T
    vir = flat(vir_ref).astype(f32)
    for place, j in enumerate(columns):
        high, low = high_low(jnp.where(meta[:, place : place + 1] == vir, held_ref[j], 0.0))
        high_ref[place * BLOCK : (place + 1) * BLOCK, :] = high
        low_ref[place * BLOCK : (place + 1) * BLOCK, :] = low


def places(j):
    return [(j >> 1) * 4 + 2 * yl + (j & 1) for yl in range(2)]


def ladder_kernel(side, near_ref, *refs):
    far_refs, (high_refs, low_refs) = refs[:SPLIT], (refs[SPLIT : SPLIT + 4 : 2], refs[SPLIT + 1 : SPLIT + 4 : 2])
    scale_ref, out_ref, *token_ref = refs[SPLIT + 4 :]
    step = 2 * COLS // SPLIT
    for ref in token_ref:
        ref[...] = jnp.zeros(ref.shape, f32)
    lines = PART * HALF
    total = None
    group = 4
    for j0 in range(0, COLS, group):
        left = [
            jnp.concatenate(
                [near_ref[e] for e in places(j)]
                + [far_refs[e // step][e % step] for e in places(j)],
                axis=0,
            )
            for j in range(j0, j0 + group)
        ]
        part, first = divmod(j0, COLS // 2)
        depth = slice(first * BLOCK, (first + group) * BLOCK)
        a_high, a_low = high_low(jnp.concatenate(left, axis=1))
        twice = mm(jnp.concatenate([a_high, a_low], axis=0), high_refs[part][depth, :])
        term = twice[:lines] + twice[lines:] + mm(a_high, low_refs[part][depth, :])
        total = term if total is None else total + term
    out_ref[...] = total * scale_ref[side * lines : (side + 1) * lines, :]


def expand_kernel(side, own_ref, other_ref, rows_ref, vir_ref, *refs):
    out_ref, held, sems = refs[-3:]
    upper = lax.axis_index("yh")
    lane = iota((1, 2 * SLOTS), 1)
    mine = (lane & HALF) == 0
    wanted = rank_of(lane & 15, jnp.where(mine, upper, 1 - upper)).astype(f32)
    sign = jnp.where(mine, 1.0, -1.0)
    vir = flat(vir_ref).astype(f32)
    copies = []
    for r in range(PART):
        slots = slice(r * HALF, (r + 1) * HALF)
        i = side * PART + r
        packed = jnp.concatenate([own_ref[slots, :], other_ref[slots, :]], axis=0)
        high, low = high_low(packed)
        pick = jnp.where(rows_ref[:, BLOCKS + i : BLOCKS + i + 1] == wanted, sign, 0.0).astype(bf16)
        spread = mm(pick, jnp.concatenate([high, low], axis=0))
        spread = jnp.where(rows_ref[:, i : i + 1] == vir, spread, 0.0)
        held[0, r] = spread
        held[1, r] = -spread
        for mirror in range(2):
            copies.append(
                pltpu.make_async_copy(
                    held.at[mirror, r], out_ref.at[mirror, other_block(i)], sems.at[mirror, r]
                )
            )
            copies[-1].start()
    for copy in copies:
        copy.wait()


def join_kernel(in_ref, after_ref, out_ref):
    pass


VMEM = pl.BlockSpec(memory_space=pltpu.VMEM)
SMEM = pl.BlockSpec(memory_space=pltpu.SMEM)
ANY = pl.BlockSpec(memory_space=pl.ANY)
HBM = pl.BlockSpec(memory_space=pltpu.HBM)


SMALL = pl.CostEstimate(flops=1000, bytes_accessed=1000, transcendentals=0)


def params(mib):
    return pltpu.CompilerParams(vmem_limit_bytes=mib * MIB)


def swapped(x, *axes):
    axes = tuple(sorted(axes, key=(ROW + COL).index))
    count = 1 << len(axes)
    return lax.ppermute(x, axes, [(i, count - 1 - i) for i in range(count)])


def core_swapped(x, token=None):
    parts = jnp.split(x, SPLIT)
    if token is not None:
        parts = [jnp.concatenate([part, token], axis=0) for part in parts]
    return [swapped(part, "core") for part in parts]


def one_pass(base, amplitudes, integrals, occ, cd, vir, energy, vir_energy):
    depth, width = integrals.shape
    shape = jax.ShapeDtypeStruct
    token = shape((1, HALF, BLOCK), f32)
    packed = pl.pallas_call(
        pack_kernel,
        out_shape=shape((8, HALF + META, BLOCK), f32),
        in_specs=[SMEM, VMEM, VMEM, VMEM],
        out_specs=VMEM,
        compiler_params=params(8),
    )(base, amplitudes, occ, cd)
    scale, rows, listed, passes = pl.pallas_call(
        table_kernel,
        out_shape=[
            shape((BLOCKS * HALF, width), f32),
            shape((BLOCK, BLOCK), f32),
            token,
            shape((1,), i32),
        ],
        in_specs=[SMEM, VMEM, VMEM, VMEM, VMEM],
        out_specs=[VMEM, VMEM, VMEM, SMEM],
        compiler_params=params(8),
        cost_estimate=SMALL,
    )(base, occ, energy, vir, vir_energy)

    v, loaded = pl.pallas_call(
        load_kernel,
        out_shape=[shape((COLS, BLOCK, width), f32), token],
        in_specs=[HBM],
        out_specs=[VMEM] * 2,
        scratch_shapes=[pltpu.SemaphoreType.DMA((COLS,))],
        compiler_params=params(8),
        cost_estimate=SMALL,
    )(integrals)

    met = lax.all_to_all(packed, NEAR, 0, 0, tiled=True)
    met = met[:4] + met[4:]
    x = met[:, :HALF].reshape(-1, BLOCK)
    meta = (met[:2, HALF:] + met[2:, HALF:]).reshape(-1, BLOCK)
    def split(part, meta):
        return pl.pallas_call(
            functools.partial(split_kernel, part),
            out_shape=[shape((depth // 2, width), bf16), shape((depth // 2, width), bf16), token],
            in_specs=[VMEM] * 3,
            out_specs=[VMEM] * 3,
            compiler_params=params(24),
            cost_estimate=SMALL,
        )(meta, vir, v)

    for step, token_done in zip(COL_STEPS, (listed, loaded, None)):
        there = swapped(jnp.concatenate([x, meta], axis=0), *step)
        meta = meta + there[x.shape[0] :]
        x = jnp.concatenate([x, there[: x.shape[0]]], axis=0)
        if token_done is not None:
            known = meta
            meta = meta + token_done[0]
    x = x.reshape(-1, HALF, BLOCK)
    *early, early_token = split(0, known)
    beyond = swapped(jnp.concatenate([x, early_token], axis=0), *X_STEP)[:-1]
    near = core_swapped(x)
    *late, late_token = split(1, meta)

    def ladder(side, near, far):
        return pl.pallas_call(
            functools.partial(ladder_kernel, side),
            out_shape=[shape((PART * HALF, width), f32)] + [token] * (1 - side),
            in_specs=[VMEM] * (6 + SPLIT),
            out_specs=[VMEM] * (2 - side),
            compiler_params=params(24),
            cost_estimate=SMALL,
        )(near, *far, *early, *late, scale)

    def expand(side, own, other, *out):
        return pl.pallas_call(
            functools.partial(expand_kernel, side),
            out_shape=pltpu.HBM((2, BLOCKS, BLOCK, width), f32),
            in_specs=[VMEM] * 4 + [HBM] * len(out),
            out_specs=HBM,
            scratch_shapes=[
                pltpu.VMEM((2, PART, BLOCK, width), f32),
                pltpu.SemaphoreType.DMA((2, PART)),
            ],
            input_output_aliases={4: 0} if out else {},
            compiler_params=params(24),
            cost_estimate=SMALL,
        )(own, other, rows, vir, *out)

    first, done = ladder(0, x, near)
    first_met = swapped(first, "yh")
    (second,) = ladder(1, beyond, core_swapped(beyond, done + late_token))
    second = pl.pallas_call(
        join_kernel,
        out_shape=shape(second.shape, f32),
        in_specs=[ANY, ANY],
        out_specs=ANY,
        input_output_aliases={0: 0},
        compiler_params=params(8),
        cost_estimate=SMALL,
    )(second, first_met)
    second_met = swapped(second, "yh")
    out = expand(0, first, first_met)
    out = expand(1, second, second_met, out)
    return out, passes[0]


def local(amplitudes, integrals, occ_irrep, cd_irrep, vir_irrep, occ_energy, vir_energy):
    run = functools.partial(
        one_pass,
        amplitudes=amplitudes,
        integrals=integrals,
        occ=occ_irrep.reshape(-1, BLOCK),
        cd=cd_irrep.reshape(1, -1),
        vir=vir_irrep.reshape(-1, BLOCK),
        energy=occ_energy.reshape(-1, BLOCK),
        vir_energy=vir_energy.reshape(-1, BLOCK),
    )
    out, passes = run(jnp.zeros((1,), i32))

    def step(state):
        index, total = state
        extra, _ = run(jnp.full((1,), index, i32))
        return index + 1, total + extra

    def further(total):
        return lax.while_loop(lambda state: state[0] < passes, step, (jnp.int32(1), total))[1]

    out = lax.cond(passes > 1, further, lambda total: total, out)
    return out.reshape(occ_irrep.shape[0], -1)


def solution(mesh):
    bits = Mesh(mesh.devices.reshape((2,) * 8), ROW + COL)
    in_specs = (
        P(ROW, COL),
        P(None, ROW + COL),
        P(),
        P(COL),
        P(ROW + COL),
        P(),
        P(ROW + COL),
    )
    out_specs = P(None, ROW + COL)
    return jax.shard_map(local, mesh=bits, in_specs=in_specs, out_specs=out_specs, check_vma=False)
```

```python
import functools

import jax
import jax.numpy as jnp
from jax import lax
from jax.experimental import pallas as pl
from jax.experimental.pallas import tpu as pltpu
from jax.sharding import Mesh
from jax.sharding import PartitionSpec as P

BLOCK = 128
IRREPS = 8
HALF = 16
META = 8
SLOTS = 2 * HALF
BLOCKS = 8
COLS = 16
PART = BLOCKS // 2
SPLIT = 2

ROW = ("yh", "yl", "xh", "core")
COL = ("xl", "z2", "z1", "z0")

NEAR = ("yh", "yl", "xl")
COL_STEPS = (("z2", "z1"), ("z1",), ("z0",))
X_STEP = ("xh", "xl")

f32, bf16, i32 = jnp.float32, jnp.bfloat16, jnp.int32
MIB = 1 << 20


def iota(shape, dim):
    return lax.broadcasted_iota(i32, shape, dim)


def strict_upper():
    return jnp.where(iota((BLOCK, BLOCK), 0) < iota((BLOCK, BLOCK), 1), 1.0, 0.0).astype(bf16)


def mm(a, b):
    return jnp.dot(a, b, preferred_element_type=f32)


def high_low(x):
    high = x.astype(bf16)
    return high, (x - high.astype(f32)).astype(bf16)


def number(axes):
    total = 0
    for axis in axes:
        total = 2 * total + lax.axis_index(axis)
    return total


def own_block():
    return number(ROW[1:])


def other_block(index):
    xh = lax.axis_index("xh") ^ (index >> 2)
    core = lax.axis_index("core") ^ (index >> 1 & 1)
    return (index & 1) * 4 + xh * 2 + core


def other_col(index):
    mask = 0
    for place, step in enumerate(COL_STEPS):
        if index >> 1 + place & 1:
            mask ^= sum(1 << (len(COL) - 1 - COL.index(axis)) for axis in step)
    return (index & 1) * 8 + (number(COL[1:]) ^ mask)


def rank_of(slot, upper):
    return 2 * slot + upper


def flat(ref):
    return jnp.concatenate([ref[i : i + 1, :] for i in range(ref.shape[0])], axis=1)


def pack_kernel(base_ref, amp_ref, occ_ref, cd_ref, out_ref):
    upper = lax.axis_index("yh")
    y = number(("yh", "yl"))
    occ = occ_ref[pl.ds(own_block(), 1), :]
    same = jnp.where(occ == iota((IRREPS, BLOCK), 0), 1.0, 0.0)
    ranks = mm(same.astype(bf16), strict_upper())
    rank = jnp.sum(same * ranks, axis=0, keepdims=True).astype(i32)
    key = occ * BLOCK + rank - base_ref[0] * SLOTS
    line = iota((2 * BLOCK, BLOCK), 0)
    wanted = ((line >> 4) & 7) * BLOCK + rank_of(line & 15, line >> 7)
    pick = jnp.where(key == wanted, 1.0, 0.0).astype(bf16)
    amp = amp_ref[...]
    first = amp.astype(bf16)
    rest = amp - first.astype(f32)
    second = rest.astype(bf16)
    packed = mm(pick, first) + mm(pick, second)
    cd = cd_ref[...]
    sign = (1 - 2 * upper).astype(f32)
    tile = jnp.where(iota((META, BLOCK), 0) == number(COL[1:]), cd.astype(f32), 0.0)
    for side in range(2):
        total = jnp.zeros((HALF, BLOCK), f32)
        for g in range(IRREPS):
            lines = packed[side * BLOCK + g * HALF : side * BLOCK + (g + 1) * HALF]
            total = total + jnp.where(cd == g, lines, 0.0)
        total = sign * total
        for yl in range(2):
            mine = jnp.where(y == 2 * side + yl, tile, 0.0)
            for xl in range(2):
                place = 4 * side + 2 * yl + xl
                out_ref[place, :HALF, :] = total
                out_ref[place, HALF:, :] = mine


def table_kernel(
    base_ref, occ_ref, energy_ref, vir_ref, vir_energy_ref, scale_ref, rows_ref, token_ref, passes_ref
):
    token_ref[...] = jnp.zeros(token_ref.shape, f32)
    upper = lax.axis_index("yh")

    def ordered(ref):
        return jnp.concatenate(
            [ref[pl.ds(other_block(i), 1), :] for i in range(BLOCKS)], axis=0
        )

    occ = ordered(occ_ref)
    energy = ordered(energy_ref)
    irrep = iota((IRREPS, BLOCK), 0)
    same = jnp.concatenate(
        [jnp.where(occ[b : b + 1] == irrep, 1.0, 0.0) for b in range(BLOCKS)], axis=0
    )
    ranks = mm(same.astype(bf16), strict_upper())
    counts = jnp.sum(same, axis=1, keepdims=True)
    most = jnp.max(counts).astype(i32)
    passes_ref[0] = (most + SLOTS - 1) // SLOTS
    rank = jnp.concatenate(
        [
            jnp.sum((same * ranks)[b * IRREPS : (b + 1) * IRREPS], axis=0, keepdims=True)
            for b in range(BLOCKS)
        ],
        axis=0,
    ).astype(i32) - base_ref[0] * SLOTS
    both = jnp.concatenate(
        [occ.astype(f32), rank.astype(f32), jnp.zeros((BLOCK - 2 * BLOCKS, BLOCK), f32)], axis=0
    )
    rows_ref[...] = both.T
    key = occ * BLOCK + rank
    line = iota((BLOCK, BLOCK), 0)
    wanted = (line >> 4) * BLOCK + rank_of(line & 15, upper)
    vir = flat(vir_ref)
    vir_energy = flat(vir_energy_ref)
    for b in range(BLOCKS):
        found = jnp.sum(
            jnp.where(key[b : b + 1] == wanted, energy[b : b + 1], 0.0), axis=1, keepdims=True
        )
        at_slot = jnp.zeros((HALF, vir.shape[1]), f32)
        for g in range(IRREPS):
            at_slot = at_slot + jnp.where(vir == g, found[g * HALF : (g + 1) * HALF], 0.0)
        scale_ref[b * HALF : (b + 1) * HALF, :] = 0.5 / (at_slot - vir_energy)


def load_kernel(v_ref, out_ref, token_ref, sems):
    token_ref[...] = jnp.zeros(token_ref.shape, f32)
    copies = []
    for j in range(COLS):
        start = pl.multiple_of(other_col(j) * BLOCK, BLOCK)
        copies.append(pltpu.make_async_copy(v_ref.at[pl.ds(start, BLOCK)], out_ref.at[j], sems.at[j]))
        copies[-1].start()
    for copy in copies:
        copy.wait()


def split_kernel(part, meta_ref, vir_ref, held_ref, high_ref, low_ref, token_ref):
    token_ref[...] = jnp.zeros(token_ref.shape, f32)
    columns = range(part * (COLS // 2), (part + 1) * (COLS // 2))
    meta = jnp.concatenate(
        [meta_ref[pl.ds(other_col(j), 1), :] for j in columns]
        + [jnp.zeros((BLOCK - COLS // 2, BLOCK), f32)],
        axis=0,
    ).T
    vir = flat(vir_ref).astype(f32)
    for place, j in enumerate(columns):
        high, low = high_low(jnp.where(meta[:, place : place + 1] == vir, held_ref[j], 0.0))
        high_ref[place * BLOCK : (place + 1) * BLOCK, :] = high
        low_ref[place * BLOCK : (place + 1) * BLOCK, :] = low


def places(j):
    return [(j >> 1) * 4 + 2 * yl + (j & 1) for yl in range(2)]


def ladder_kernel(side, near_ref, *refs):
    far_refs, (high_refs, low_refs) = refs[:SPLIT], (refs[SPLIT : SPLIT + 4 : 2], refs[SPLIT + 1 : SPLIT + 4 : 2])
    scale_ref, out_ref, *token_ref = refs[SPLIT + 4 :]
    step = 2 * COLS // SPLIT
    for ref in token_ref:
        ref[...] = jnp.zeros(ref.shape, f32)
    lines = PART * HALF
    total = None
    group = 8
    for j0 in range(0, COLS, group):
        left = [
            jnp.concatenate(
                [near_ref[e] for e in places(j)]
                + [far_refs[e // step][e % step] for e in places(j)],
                axis=0,
            )
            for j in range(j0, j0 + group)
        ]
        part, first = divmod(j0, COLS // 2)
        depth = slice(first * BLOCK, (first + group) * BLOCK)
        a_high, a_low = high_low(jnp.concatenate(left, axis=1))
        twice = mm(jnp.concatenate([a_high, a_low], axis=0), high_refs[part][depth, :])
        term = twice[:lines] + twice[lines:] + mm(a_high, low_refs[part][depth, :])
        total = term if total is None else total + term
    out_ref[...] = total * scale_ref[side * lines : (side + 1) * lines, :]


def expand_kernel(side, own_ref, other_ref, rows_ref, vir_ref, *refs):
    out_ref, held, sems = refs[-3:]
    upper = lax.axis_index("yh")
    lane = iota((1, 2 * SLOTS), 1)
    mine = (lane & HALF) == 0
    wanted = rank_of(lane & 15, jnp.where(mine, upper, 1 - upper)).astype(f32)
    sign = jnp.where(mine, 1.0, -1.0)
    vir = flat(vir_ref).astype(f32)
    copies = []
    for r in range(PART):
        slots = slice(r * HALF, (r + 1) * HALF)
        i = side * PART + r
        packed = jnp.concatenate([own_ref[slots, :], other_ref[slots, :]], axis=0)
        high, low = high_low(packed)
        pick = jnp.where(rows_ref[:, BLOCKS + i : BLOCKS + i + 1] == wanted, sign, 0.0).astype(bf16)
        spread = mm(pick, jnp.concatenate([high, low], axis=0))
        spread = jnp.where(rows_ref[:, i : i + 1] == vir, spread, 0.0)
        held[0, r] = spread
        held[1, r] = -spread
        for mirror in range(2):
            copies.append(
                pltpu.make_async_copy(
                    held.at[mirror, r], out_ref.at[mirror, other_block(i)], sems.at[mirror, r]
                )
            )
            copies[-1].start()
    for copy in copies:
        copy.wait()


def join_kernel(in_ref, after_ref, out_ref):
    pass


VMEM = pl.BlockSpec(memory_space=pltpu.VMEM)
SMEM = pl.BlockSpec(memory_space=pltpu.SMEM)
ANY = pl.BlockSpec(memory_space=pl.ANY)
HBM = pl.BlockSpec(memory_space=pltpu.HBM)


SMALL = pl.CostEstimate(flops=1000, bytes_accessed=1000, transcendentals=0)


def params(mib):
    return pltpu.CompilerParams(vmem_limit_bytes=mib * MIB)


def swapped(x, *axes):
    axes = tuple(sorted(axes, key=(ROW + COL).index))
    count = 1 << len(axes)
    return lax.ppermute(x, axes, [(i, count - 1 - i) for i in range(count)])


def core_swapped(x, token=None):
    parts = jnp.split(x, SPLIT)
    if token is not None:
        parts = [jnp.concatenate([part, token], axis=0) for part in parts]
    return [swapped(part, "core") for part in parts]


def one_pass(base, amplitudes, integrals, occ, cd, vir, energy, vir_energy):
    depth, width = integrals.shape
    shape = jax.ShapeDtypeStruct
    token = shape((1, HALF, BLOCK), f32)
    packed = pl.pallas_call(
        pack_kernel,
        out_shape=shape((8, HALF + META, BLOCK), f32),
        in_specs=[SMEM, VMEM, VMEM, VMEM],
        out_specs=VMEM,
        compiler_params=params(8),
    )(base, amplitudes, occ, cd)
    scale, rows, listed, passes = pl.pallas_call(
        table_kernel,
        out_shape=[
            shape((BLOCKS * HALF, width), f32),
            shape((BLOCK, BLOCK), f32),
            token,
            shape((1,), i32),
        ],
        in_specs=[SMEM, VMEM, VMEM, VMEM, VMEM],
        out_specs=[VMEM, VMEM, VMEM, SMEM],
        compiler_params=params(8),
        cost_estimate=SMALL,
    )(base, occ, energy, vir, vir_energy)

    v, loaded = pl.pallas_call(
        load_kernel,
        out_shape=[shape((COLS, BLOCK, width), f32), token],
        in_specs=[HBM],
        out_specs=[VMEM] * 2,
        scratch_shapes=[pltpu.SemaphoreType.DMA((COLS,))],
        compiler_params=params(8),
        cost_estimate=SMALL,
    )(integrals)

    met = lax.all_to_all(packed, NEAR, 0, 0, tiled=True)
    met = met[:4] + met[4:]
    x = met[:, :HALF].reshape(-1, BLOCK)
    meta = (met[:2, HALF:] + met[2:, HALF:]).reshape(-1, BLOCK)
    def split(part, meta):
        return pl.pallas_call(
            functools.partial(split_kernel, part),
            out_shape=[shape((depth // 2, width), bf16), shape((depth // 2, width), bf16), token],
            in_specs=[VMEM] * 3,
            out_specs=[VMEM] * 3,
            compiler_params=params(24),
            cost_estimate=SMALL,
        )(meta, vir, v)

    for step, token_done in zip(COL_STEPS, (listed, loaded, None)):
        there = swapped(jnp.concatenate([x, meta], axis=0), *step)
        meta = meta + there[x.shape[0] :]
        x = jnp.concatenate([x, there[: x.shape[0]]], axis=0)
        if token_done is not None:
            known = meta
            meta = meta + token_done[0]
    x = x.reshape(-1, HALF, BLOCK)
    *early, early_token = split(0, known)
    beyond = swapped(jnp.concatenate([x, early_token], axis=0), *X_STEP)[:-1]
    near = core_swapped(x)
    *late, late_token = split(1, meta)

    def ladder(side, near, far):
        return pl.pallas_call(
            functools.partial(ladder_kernel, side),
            out_shape=[shape((PART * HALF, width), f32)] + [token] * (1 - side),
            in_specs=[VMEM] * (6 + SPLIT),
            out_specs=[VMEM] * (2 - side),
            compiler_params=params(24),
            cost_estimate=SMALL,
        )(near, *far, *early, *late, scale)

    def expand(side, own, other, *out):
        return pl.pallas_call(
            functools.partial(expand_kernel, side),
            out_shape=pltpu.HBM((2, BLOCKS, BLOCK, width), f32),
            in_specs=[VMEM] * 4 + [HBM] * len(out),
            out_specs=HBM,
            scratch_shapes=[
                pltpu.VMEM((2, PART, BLOCK, width), f32),
                pltpu.SemaphoreType.DMA((2, PART)),
            ],
            input_output_aliases={4: 0} if out else {},
            compiler_params=params(24),
            cost_estimate=SMALL,
        )(own, other, rows, vir, *out)

    first, done = ladder(0, x, near)
    first_met = swapped(first, "yh")
    (second,) = ladder(1, beyond, core_swapped(beyond, done + late_token))
    second = pl.pallas_call(
        join_kernel,
        out_shape=shape(second.shape, f32),
        in_specs=[ANY, ANY],
        out_specs=ANY,
        input_output_aliases={0: 0},
        compiler_params=params(8),
        cost_estimate=SMALL,
    )(second, first_met)
    second_met = swapped(second, "yh")
    out = expand(0, first, first_met)
    out = expand(1, second, second_met, out)
    return out, passes[0]


def local(amplitudes, integrals, occ_irrep, cd_irrep, vir_irrep, occ_energy, vir_energy):
    run = functools.partial(
        one_pass,
        amplitudes=amplitudes,
        integrals=integrals,
        occ=occ_irrep.reshape(-1, BLOCK),
        cd=cd_irrep.reshape(1, -1),
        vir=vir_irrep.reshape(-1, BLOCK),
        energy=occ_energy.reshape(-1, BLOCK),
        vir_energy=vir_energy.reshape(-1, BLOCK),
    )
    out, passes = run(jnp.zeros((1,), i32))

    def step(state):
        index, total = state
        extra, _ = run(jnp.full((1,), index, i32))
        return index + 1, total + extra

    def further(total):
        return lax.while_loop(lambda state: state[0] < passes, step, (jnp.int32(1), total))[1]

    out = lax.cond(passes > 1, further, lambda total: total, out)
    return out.reshape(occ_irrep.shape[0], -1)


def solution(mesh):
    bits = Mesh(mesh.devices.reshape((2,) * 8), ROW + COL)
    in_specs = (
        P(ROW, COL),
        P(None, ROW + COL),
        P(),
        P(COL),
        P(ROW + COL),
        P(),
        P(ROW + COL),
    )
    out_specs = P(None, ROW + COL)
    return jax.shard_map(local, mesh=bits, in_specs=in_specs, out_specs=out_specs, check_vma=False)
```

```python
import functools

import jax
import jax.numpy as jnp
from jax import lax
from jax.experimental import pallas as pl
from jax.experimental.pallas import tpu as pltpu
from jax.sharding import Mesh
from jax.sharding import PartitionSpec as P

BLOCK = 128
IRREPS = 8
HALF = 16
META = 8
SLOTS = 2 * HALF
BLOCKS = 8
COLS = 16
PART = BLOCKS // 2
SPLIT = 2

ROW = ("yh", "yl", "xh", "core")
COL = ("xl", "z2", "z1", "z0")

NEAR = ("yh", "yl", "xl")
COL_STEPS = (("z2", "z1"), ("z1",), ("z0",))
X_STEP = ("xh",)

f32, bf16, i32 = jnp.float32, jnp.bfloat16, jnp.int32
MIB = 1 << 20


def iota(shape, dim):
    return lax.broadcasted_iota(i32, shape, dim)


def strict_upper():
    return jnp.where(iota((BLOCK, BLOCK), 0) < iota((BLOCK, BLOCK), 1), 1.0, 0.0).astype(bf16)


def mm(a, b):
    return jnp.dot(a, b, preferred_element_type=f32)


def high_low(x):
    high = x.astype(bf16)
    return high, (x - high.astype(f32)).astype(bf16)


def number(axes):
    total = 0
    for axis in axes:
        total = 2 * total + lax.axis_index(axis)
    return total


def own_block():
    return number(ROW[1:])


def other_block(index):
    xh = lax.axis_index("xh") ^ (index >> 2)
    core = lax.axis_index("core") ^ (index >> 1 & 1)
    return (index & 1) * 4 + xh * 2 + core


def other_col(index):
    mask = 0
    for place, step in enumerate(COL_STEPS):
        if index >> 1 + place & 1:
            mask ^= sum(1 << (len(COL) - 1 - COL.index(axis)) for axis in step)
    return (index & 1) * 8 + (number(COL[1:]) ^ mask)


def rank_of(slot, upper):
    return 2 * slot + upper


def flat(ref):
    return jnp.concatenate([ref[i : i + 1, :] for i in range(ref.shape[0])], axis=1)


def pack_kernel(base_ref, amp_ref, occ_ref, cd_ref, out_ref):
    upper = lax.axis_index("yh")
    y = number(("yh", "yl"))
    occ = occ_ref[pl.ds(own_block(), 1), :]
    same = jnp.where(occ == iota((IRREPS, BLOCK), 0), 1.0, 0.0)
    ranks = mm(same.astype(bf16), strict_upper())
    rank = jnp.sum(same * ranks, axis=0, keepdims=True).astype(i32)
    key = occ * BLOCK + rank - base_ref[0] * SLOTS
    line = iota((2 * BLOCK, BLOCK), 0)
    wanted = ((line >> 4) & 7) * BLOCK + rank_of(line & 15, line >> 7)
    pick = jnp.where(key == wanted, 1.0, 0.0).astype(bf16)
    amp = amp_ref[...]
    first = amp.astype(bf16)
    rest = amp - first.astype(f32)
    second = rest.astype(bf16)
    packed = mm(pick, first) + mm(pick, second)
    cd = cd_ref[...]
    sign = (1 - 2 * upper).astype(f32)
    tile = jnp.where(iota((META, BLOCK), 0) == number(COL[1:]), cd.astype(f32), 0.0)
    for side in range(2):
        total = jnp.zeros((HALF, BLOCK), f32)
        for g in range(IRREPS):
            lines = packed[side * BLOCK + g * HALF : side * BLOCK + (g + 1) * HALF]
            total = total + jnp.where(cd == g, lines, 0.0)
        total = sign * total
        for yl in range(2):
            mine = jnp.where(y == 2 * side + yl, tile, 0.0)
            for xl in range(2):
                place = 4 * side + 2 * yl + xl
                out_ref[place, :HALF, :] = total
                out_ref[place, HALF:, :] = mine


def table_kernel(
    base_ref, occ_ref, energy_ref, vir_ref, vir_energy_ref, scale_ref, rows_ref, token_ref, passes_ref
):
    token_ref[...] = jnp.zeros(token_ref.shape, f32)
    upper = lax.axis_index("yh")

    def ordered(ref):
        return jnp.concatenate(
            [ref[pl.ds(other_block(i), 1), :] for i in range(BLOCKS)], axis=0
        )

    occ = ordered(occ_ref)
    energy = ordered(energy_ref)
    irrep = iota((IRREPS, BLOCK), 0)
    same = jnp.concatenate(
        [jnp.where(occ[b : b + 1] == irrep, 1.0, 0.0) for b in range(BLOCKS)], axis=0
    )
    ranks = mm(same.astype(bf16), strict_upper())
    counts = jnp.sum(same, axis=1, keepdims=True)
    most = jnp.max(counts).astype(i32)
    passes_ref[0] = (most + SLOTS - 1) // SLOTS
    rank = jnp.concatenate(
        [
            jnp.sum((same * ranks)[b * IRREPS : (b + 1) * IRREPS], axis=0, keepdims=True)
            for b in range(BLOCKS)
        ],
        axis=0,
    ).astype(i32) - base_ref[0] * SLOTS
    both = jnp.concatenate(
        [occ.astype(f32), rank.astype(f32), jnp.zeros((BLOCK - 2 * BLOCKS, BLOCK), f32)], axis=0
    )
    rows_ref[...] = both.T
    key = occ * BLOCK + rank
    line = iota((BLOCK, BLOCK), 0)
    wanted = (line >> 4) * BLOCK + rank_of(line & 15, upper)
    vir = flat(vir_ref)
    vir_energy = flat(vir_energy_ref)
    for b in range(BLOCKS):
        found = jnp.sum(
            jnp.where(key[b : b + 1] == wanted, energy[b : b + 1], 0.0), axis=1, keepdims=True
        )
        at_slot = jnp.zeros((HALF, vir.shape[1]), f32)
        for g in range(IRREPS):
            at_slot = at_slot + jnp.where(vir == g, found[g * HALF : (g + 1) * HALF], 0.0)
        scale_ref[b * HALF : (b + 1) * HALF, :] = 0.5 / (at_slot - vir_energy)


def load_kernel(v_ref, out_ref, token_ref, sems):
    token_ref[...] = jnp.zeros(token_ref.shape, f32)
    copies = []
    for j in range(COLS):
        start = pl.multiple_of(other_col(j) * BLOCK, BLOCK)
        copies.append(pltpu.make_async_copy(v_ref.at[pl.ds(start, BLOCK)], out_ref.at[j], sems.at[j]))
        copies[-1].start()
    for copy in copies:
        copy.wait()


def split_kernel(part, meta_ref, vir_ref, held_ref, high_ref, low_ref, token_ref):
    token_ref[...] = jnp.zeros(token_ref.shape, f32)
    columns = range(part * (COLS // 2), (part + 1) * (COLS // 2))
    meta = jnp.concatenate(
        [meta_ref[pl.ds(other_col(j), 1), :] for j in columns]
        + [jnp.zeros((BLOCK - COLS // 2, BLOCK), f32)],
        axis=0,
    ).T
    vir = flat(vir_ref).astype(f32)
    for place, j in enumerate(columns):
        high, low = high_low(jnp.where(meta[:, place : place + 1] == vir, held_ref[j], 0.0))
        high_ref[place * BLOCK : (place + 1) * BLOCK, :] = high
        low_ref[place * BLOCK : (place + 1) * BLOCK, :] = low


def places(j):
    return [(j >> 1) * 4 + 2 * yl + (j & 1) for yl in range(2)]


def ladder_kernel(side, near_ref, *refs):
    far_refs, (high_refs, low_refs) = refs[:SPLIT], (refs[SPLIT : SPLIT + 4 : 2], refs[SPLIT + 1 : SPLIT + 4 : 2])
    scale_ref, out_ref, *token_ref = refs[SPLIT + 4 :]
    step = 2 * COLS // SPLIT
    for ref in token_ref:
        ref[...] = jnp.zeros(ref.shape, f32)
    lines = PART * HALF
    total = None
    group = 4
    for j0 in range(0, COLS, group):
        left = [
            jnp.concatenate(
                [near_ref[e] for e in places(j)]
                + [far_refs[e // step][e % step] for e in places(j)],
                axis=0,
            )
            for j in range(j0, j0 + group)
        ]
        part, first = divmod(j0, COLS // 2)
        depth = slice(first * BLOCK, (first + group) * BLOCK)
        a_high, a_low = high_low(jnp.concatenate(left, axis=1))
        twice = mm(jnp.concatenate([a_high, a_low], axis=0), high_refs[part][depth, :])
        term = twice[:lines] + twice[lines:] + mm(a_high, low_refs[part][depth, :])
        total = term if total is None else total + term
    out_ref[...] = total * scale_ref[side * lines : (side + 1) * lines, :]


def expand_kernel(side, own_ref, other_ref, rows_ref, vir_ref, *refs):
    out_ref, held, sems = refs[-3:]
    upper = lax.axis_index("yh")
    lane = iota((1, 2 * SLOTS), 1)
    mine = (lane & HALF) == 0
    wanted = rank_of(lane & 15, jnp.where(mine, upper, 1 - upper)).astype(f32)
    sign = jnp.where(mine, 1.0, -1.0)
    vir = flat(vir_ref).astype(f32)
    copies = []
    for r in range(PART):
        slots = slice(r * HALF, (r + 1) * HALF)
        i = side * PART + r
        packed = jnp.concatenate([own_ref[slots, :], other_ref[slots, :]], axis=0)
        high, low = high_low(packed)
        pick = jnp.where(rows_ref[:, BLOCKS + i : BLOCKS + i + 1] == wanted, sign, 0.0).astype(bf16)
        spread = mm(pick, jnp.concatenate([high, low], axis=0))
        spread = jnp.where(rows_ref[:, i : i + 1] == vir, spread, 0.0)
        held[0, r] = spread
        held[1, r] = -spread
        for mirror in range(2):
            copies.append(
                pltpu.make_async_copy(
                    held.at[mirror, r], out_ref.at[mirror, other_block(i)], sems.at[mirror, r]
                )
            )
            copies[-1].start()
    for copy in copies:
        copy.wait()


def join_kernel(in_ref, after_ref, out_ref):
    pass


VMEM = pl.BlockSpec(memory_space=pltpu.VMEM)
SMEM = pl.BlockSpec(memory_space=pltpu.SMEM)
ANY = pl.BlockSpec(memory_space=pl.ANY)
HBM = pl.BlockSpec(memory_space=pltpu.HBM)


SMALL = pl.CostEstimate(flops=1000, bytes_accessed=1000, transcendentals=0)


def params(mib):
    return pltpu.CompilerParams(vmem_limit_bytes=mib * MIB)


def swapped(x, *axes):
    axes = tuple(sorted(axes, key=(ROW + COL).index))
    count = 1 << len(axes)
    return lax.ppermute(x, axes, [(i, count - 1 - i) for i in range(count)])


def core_swapped(x, token=None):
    parts = jnp.split(x, SPLIT)
    if token is not None:
        parts = [jnp.concatenate([part, token], axis=0) for part in parts]
    return [swapped(part, "core") for part in parts]


def one_pass(base, amplitudes, integrals, occ, cd, vir, energy, vir_energy):
    depth, width = integrals.shape
    shape = jax.ShapeDtypeStruct
    token = shape((1, HALF, BLOCK), f32)
    packed = pl.pallas_call(
        pack_kernel,
        out_shape=shape((8, HALF + META, BLOCK), f32),
        in_specs=[SMEM, VMEM, VMEM, VMEM],
        out_specs=VMEM,
        compiler_params=params(8),
    )(base, amplitudes, occ, cd)
    scale, rows, listed, passes = pl.pallas_call(
        table_kernel,
        out_shape=[
            shape((BLOCKS * HALF, width), f32),
            shape((BLOCK, BLOCK), f32),
            token,
            shape((1,), i32),
        ],
        in_specs=[SMEM, VMEM, VMEM, VMEM, VMEM],
        out_specs=[VMEM, VMEM, VMEM, SMEM],
        compiler_params=params(8),
        cost_estimate=SMALL,
    )(base, occ, energy, vir, vir_energy)

    v, loaded = pl.pallas_call(
        load_kernel,
        out_shape=[shape((COLS, BLOCK, width), f32), token],
        in_specs=[HBM],
        out_specs=[VMEM] * 2,
        scratch_shapes=[pltpu.SemaphoreType.DMA((COLS,))],
        compiler_params=params(8),
        cost_estimate=SMALL,
    )(integrals)

    met = lax.all_to_all(packed, NEAR, 0, 0, tiled=True)
    met = met[:4] + met[4:]
    x = met[:, :HALF].reshape(-1, BLOCK)
    meta = (met[:2, HALF:] + met[2:, HALF:]).reshape(-1, BLOCK)
    def split(part, meta):
        return pl.pallas_call(
            functools.partial(split_kernel, part),
            out_shape=[shape((depth // 2, width), bf16), shape((depth // 2, width), bf16), token],
            in_specs=[VMEM] * 3,
            out_specs=[VMEM] * 3,
            compiler_params=params(24),
            cost_estimate=SMALL,
        )(meta, vir, v)

    for step, token_done in zip(COL_STEPS, (listed, loaded, None)):
        there = swapped(jnp.concatenate([x, meta], axis=0), *step)
        meta = meta + there[x.shape[0] :]
        x = jnp.concatenate([x, there[: x.shape[0]]], axis=0)
        if token_done is not None:
            known = meta
            meta = meta + token_done[0]
    x = x.reshape(-1, HALF, BLOCK)
    *early, early_token = split(0, known)
    beyond = swapped(jnp.concatenate([x, early_token], axis=0), *X_STEP)[:-1]
    near = core_swapped(x)
    *late, late_token = split(1, meta)

    def ladder(side, near, far):
        return pl.pallas_call(
            functools.partial(ladder_kernel, side),
            out_shape=[shape((PART * HALF, width), f32)] + [token] * (1 - side),
            in_specs=[VMEM] * (6 + SPLIT),
            out_specs=[VMEM] * (2 - side),
            compiler_params=params(24),
            cost_estimate=SMALL,
        )(near, *far, *early, *late, scale)

    def expand(side, own, other, *out):
        return pl.pallas_call(
            functools.partial(expand_kernel, side),
            out_shape=pltpu.HBM((2, BLOCKS, BLOCK, width), f32),
            in_specs=[VMEM] * 4 + [HBM] * len(out),
            out_specs=HBM,
            scratch_shapes=[
                pltpu.VMEM((2, PART, BLOCK, width), f32),
                pltpu.SemaphoreType.DMA((2, PART)),
            ],
            input_output_aliases={4: 0} if out else {},
            compiler_params=params(24),
            cost_estimate=SMALL,
        )(own, other, rows, vir, *out)

    first, done = ladder(0, x, near)
    first_met = swapped(first, "yh")
    (second,) = ladder(1, beyond, core_swapped(beyond, done + late_token))
    second = pl.pallas_call(
        join_kernel,
        out_shape=shape(second.shape, f32),
        in_specs=[ANY, ANY],
        out_specs=ANY,
        input_output_aliases={0: 0},
        compiler_params=params(8),
        cost_estimate=SMALL,
    )(second, first_met)
    second_met = swapped(second, "yh")
    out = expand(0, first, first_met)
    out = expand(1, second, second_met, out)
    return out, passes[0]


def local(amplitudes, integrals, occ_irrep, cd_irrep, vir_irrep, occ_energy, vir_energy):
    run = functools.partial(
        one_pass,
        amplitudes=amplitudes,
        integrals=integrals,
        occ=occ_irrep.reshape(-1, BLOCK),
        cd=cd_irrep.reshape(1, -1),
        vir=vir_irrep.reshape(-1, BLOCK),
        energy=occ_energy.reshape(-1, BLOCK),
        vir_energy=vir_energy.reshape(-1, BLOCK),
    )
    out, passes = run(jnp.zeros((1,), i32))

    def step(state):
        index, total = state
        extra, _ = run(jnp.full((1,), index, i32))
        return index + 1, total + extra

    def further(total):
        return lax.while_loop(lambda state: state[0] < passes, step, (jnp.int32(1), total))[1]

    out = lax.cond(passes > 1, further, lambda total: total, out)
    return out.reshape(occ_irrep.shape[0], -1)


def solution(mesh):
    bits = Mesh(mesh.devices.reshape((2,) * 8), ROW + COL)
    in_specs = (
        P(ROW, COL),
        P(None, ROW + COL),
        P(),
        P(COL),
        P(ROW + COL),
        P(),
        P(ROW + COL),
    )
    out_specs = P(None, ROW + COL)
    return jax.shard_map(local, mesh=bits, in_specs=in_specs, out_specs=out_specs, check_vma=False)
```
